128 devices in a mesh: row: 8 (over z, y_hi), col: 16 (over y_lo, x, core).
Axes of the slice: x: 4, y: 4 (y_hi: 2, y_lo: 2; y = y_hi * 2 + y_lo), z: 4, core: 2. Of those that a mesh axis runs over, the one named last changes fastest.
Arguments:
- basis_vectors: bfloat16 [8, 524288], P(None, ('row', 'col')), may hold values from -6 to 6
- block_values: bfloat16 [8, 16, 2048, 4096], P('row', 'col'), may hold values from -0.1875 to 0.1875
- blk_row: int32 [8, 16, 2048], P('row', 'col'), may hold values from 0 to 1023, as said below
- blk_col: int32 [8, 16, 2048], P('row', 'col'), may hold values from 0 to 511
- block_count: int32 [8, 16], P('row', 'col'), may hold values from 128 to 2048, as said below
Outputs:
- hx: float32 [8, 524288], P(None, ('row', 'col'))
The draws below stay inside these ranges and needn't reach their ends.
Inputs may be any that keep to these rules, and one draw needn't show every extreme that they name: `blk_row`: in every used or unused slot the global row block is at least the global column block named by blk_col of the same slot; a pair may be named by several slots. `block_count`: some pair's count equals 2048.
All inputs are finite; a program needn't handle non-finite values.
Results may differ from the reference program's by a relative error of at most 0.0003.
Values may be sent and summed in bfloat16 or wider, within the bound.
A program may use at most 192 MiB of HBM per device.

```python
import jax
import jax.numpy as jnp
from jax import lax

BLK = 64
NVEC = 8
VCH = 4096
CAP = 2048
BPC = 64
NBR = 1024
DIM = 524288
N_ROW = 8
N_COL = 16


def block_pattern(key):
    key_row, key_col = jax.random.split(key)
    row_id = jnp.arange(N_ROW, dtype=jnp.int32).reshape(N_ROW, 1, 1)
    col_id = jnp.arange(N_COL, dtype=jnp.int32).reshape(1, N_COL, 1)
    lowest = jnp.where(row_id == 0, col_id * BPC, 0) + jnp.zeros((N_ROW, N_COL, 1), jnp.int32)
    row_index = jax.random.randint(key_row, (N_ROW, N_COL, CAP), lowest, NBR, dtype=jnp.int32)
    global_row = (row_id * N_COL + row_index // BPC) * BPC + row_index % BPC
    quotient = global_row // BPC
    remainder = global_row % BPC
    shifted = quotient - col_id
    full_runs = jnp.clip((shifted + N_COL - 1) // N_COL, 0, N_ROW)
    matching = (shifted >= 0) & (shifted % N_COL == 0)
    allowed = full_runs * BPC + jnp.where(matching, remainder + 1, 0)
    col_index = jax.random.randint(key_col, (N_ROW, N_COL, CAP), 0, allowed, dtype=jnp.int32)
    return (row_index, col_index)


def draw_blk_row(key, part):
    row_index, col_index = block_pattern(key)
    return row_index.astype(jnp.int32)


def draw_blk_col(key, part):
    row_index, col_index = block_pattern(key)
    return col_index.astype(jnp.int32)


def draw_block_count(key, part):
    key = jax.random.fold_in(key, 7)
    key_level, key_top = jax.random.split(key)
    level = jax.random.randint(key_level, (N_ROW, N_COL), 0, 5, dtype=jnp.int32)
    counts = CAP // jnp.power(2, level)
    chosen = jax.random.randint(key_top, (), 0, N_ROW * N_COL, dtype=jnp.int32)
    flat_ids = jnp.arange(N_ROW * N_COL, dtype=jnp.int32).reshape(N_ROW, N_COL)
    return jnp.where(flat_ids == chosen, CAP, counts).astype(jnp.int32)


def shard_levels(stream_key, extent, pieces, low, largest):
    def one(axis_at, shards_of):
        steps = jax.random.uniform(jax.random.fold_in(jax.random.fold_in(stream_key, 6), axis_at), (shards_of,), jnp.float32, low / len(pieces), largest / len(pieces))
        return jnp.repeat(jnp.exp(steps), extent[axis_at] // shards_of).reshape((-1,) + (1,) * (len(extent) - axis_at - 1))

    factor_of = one(*pieces[0])
    for cut in pieces[1:]:
        factor_of = factor_of * one(*cut)
    return factor_of


def normal_values(own_key, dims, scale, limit, shards=(), kind=jnp.bfloat16):
    level = shard_levels(own_key, dims, shards, -0.22, 0.18) if shards else 1.0
    array = jax.random.normal(own_key, dims, jnp.float32) * scale * level
    return jnp.minimum(jnp.maximum(array, -limit), limit).astype(kind)


def setup_inputs(seed: int = 0) -> dict:
    arg_keys = jax.random.split(jax.random.key(seed), 6)
    return {
        "basis_vectors": normal_values(arg_keys[0], (NVEC, DIM), 1.0, 6.0, ((1, 128),)),
        "block_values": normal_values(arg_keys[1], (N_ROW, N_COL, CAP, BLK * BLK), (BLK * 16) ** -0.5, 0.1875, ((0, 8), (1, 16))),
        "blk_row": draw_blk_row(jax.random.fold_in(arg_keys[5], 71), 0),
        "blk_col": draw_blk_col(jax.random.fold_in(arg_keys[5], 71), 0),
        "block_count": draw_block_count(jax.random.fold_in(arg_keys[5], 71), 0),
    }


def reference(basis_vectors, block_values, blk_row, blk_col, block_count):
    per_piece = VCH // BLK
    block_total = DIM // BLK
    vectors = basis_vectors.astype(jnp.float32).reshape(NVEC, block_total, BLK)
    slot_ids = jnp.arange(CAP, dtype=jnp.int32)
    row_ids = jnp.repeat(jnp.arange(N_ROW, dtype=jnp.int32), N_COL)
    col_ids = jnp.tile(jnp.arange(N_COL, dtype=jnp.int32), N_ROW)
    all_values = block_values.reshape(N_ROW * N_COL, CAP, BLK * BLK)
    all_rows = blk_row.reshape(N_ROW * N_COL, CAP)
    all_cols = blk_col.reshape(N_ROW * N_COL, CAP)
    all_counts = block_count.reshape(N_ROW * N_COL)

    def add_device(accumulated, device_item):
        row_id, col_id, values, row_index, col_index, used_count = device_item
        global_row = (row_id * N_COL + row_index // per_piece) * per_piece + row_index % per_piece
        global_col = ((col_index // per_piece) * N_COL + col_id) * per_piece + col_index % per_piece
        used_slot = slot_ids < used_count
        row_target = jnp.where(used_slot, global_row, block_total)
        col_target = jnp.where(used_slot, global_col, block_total)
        matrices = values.astype(jnp.float32).reshape(CAP, BLK, BLK)
        col_vectors = jnp.take(vectors, global_col, axis=1)
        row_vectors = jnp.take(vectors, global_row, axis=1)
        forward = jnp.einsum("sik,vsk->vsi", matrices, col_vectors, precision=lax.Precision.HIGHEST)
        backward = jnp.einsum("sik,vsi->vsk", matrices, row_vectors, precision=lax.Precision.HIGHEST)
        accumulated = accumulated.at[:, row_target, :].add(forward, mode="drop")
        accumulated = accumulated.at[:, col_target, :].add(backward, mode="drop")
        return accumulated, None

    start = jnp.zeros((NVEC, block_total, BLK), jnp.float32)
    result, _ = lax.scan(add_device, start, (row_ids, col_ids, all_values, all_rows, all_cols, all_counts))
    return result.reshape(NVEC, DIM)
```

```python
import jax
import jax.numpy as jnp
from jax import lax
from jax.experimental import pallas as pl
from jax.experimental.pallas import tpu as pltpu
from jax.sharding import PartitionSpec as P

BLK = 64
NVEC = 8
PIECE = 4096
CAP = 2048
N_ROW = 8
N_COL = 16
NB_ROW = 1024
NB_COL = 512
GROUPS = CAP // 8
UNROLL = 8
F32, BF16 = jnp.float32, jnp.bfloat16
MESH = pl.DeviceIdType.MESH
SMEM = pl.BlockSpec(memory_space=pltpu.SMEM)
VMEM = pl.BlockSpec(memory_space=pltpu.VMEM)
ANY = pl.BlockSpec(memory_space=pl.ANY)
MIB = 2**20


def lane_masks():
    lane = lax.broadcasted_iota(jnp.int32, (8, 128), 1)
    return lane < 64, lane % 2 == 0


class Place:
    def __init__(self):
        self.row, self.col = lax.axis_index("row"), lax.axis_index("col")
        self.z, self.yh = self.row // 2, self.row % 2
        self.yl, self.x, self.core = self.col // 8, (self.col // 2) % 4, self.col % 2
        self.sibling = (self.row, self.col_of(self.yl, self.x, 1 - self.core))
        self.y_lo = (self.row, self.col_of(1 - self.yl, self.x, self.core))
        self.y_hi = (self.row_of(self.z, 1 - self.yh), self.col)
        self.xs = [(self.row, self.col_of(self.yl, (self.x + d) % 4, self.core)) for d in (1, 2, 3)]
        self.zs = [(self.row_of((self.z + d) % 4, self.yh), self.col) for d in (1, 2, 3)]
        self.partners = [self.sibling, self.y_lo, self.y_hi] + self.xs + self.zs

    def col_of(self, yl, x, core):
        return (yl * 4 + x) * 2 + core

    def row_of(self, z, yh):
        return z * 2 + yh

    def greet(self):
        barrier = pltpu.get_barrier_semaphore()
        for partner in self.partners:
            pl.semaphore_signal(barrier, inc=1, device_id=partner, device_id_type=MESH)

    def wait_greetings(self):
        pl.semaphore_wait(pltpu.get_barrier_semaphore(), len(self.partners))


class Sender:
    def __init__(self, sems):
        self.sems, self.sent = sems, []

    def send(self, src, dst, recv_sem, to):
        copy = pltpu.make_async_remote_copy(
            src_ref=src, dst_ref=dst, send_sem=self.sems.at[len(self.sent)], recv_sem=recv_sem,
            device_id=to, device_id_type=MESH)
        copy.start()
        self.sent.append(copy)

    def arrived(self, dst, recv_sem, place):
        pltpu.make_async_remote_copy(
            src_ref=dst, dst_ref=dst, send_sem=self.sems.at[0], recv_sem=recv_sem,
            device_id=place.sibling, device_id_type=MESH).wait_recv()

    def finish(self):
        for copy in self.sent:
            copy.wait_send()


def expand_row(src, ex, piece):
    low, even = lane_masks()

    def step(i, carry):
        for j in range(8):
            m = i * 8 + j
            x = src[:, pl.ds(pl.multiple_of(m * 128, 128), 128)].astype(F32)
            swapped = pltpu.roll(x, 64, 1)
            for h in range(2):
                d = jnp.where(low, x, swapped) if h == 0 else jnp.where(low, swapped, x)
                p0 = jnp.where(even, d, pltpu.roll(d, 1, 1))
                p1 = jnp.where(even, pltpu.roll(d, 127, 1), d)
                ex[piece * 64 + 2 * m + h] = jnp.concatenate([p0, p1], axis=0).astype(BF16)
        return carry

    lax.fori_loop(0, 4, step, 0)


def expand_col(src, xc, piece):
    low, _ = lane_masks()

    def step(i, carry):
        for j in range(8):
            m = i * 8 + j
            x = src[:, pl.ds(pl.multiple_of(m * 128, 128), 128)].astype(F32)
            swapped = pltpu.roll(x, 64, 1)
            zero = jnp.zeros_like(x)
            xc[piece * 64 + 2 * m] = jnp.concatenate([jnp.where(low, x, zero), jnp.where(low, zero, swapped)], axis=0).astype(BF16)
            xc[piece * 64 + 2 * m + 1] = jnp.concatenate([jnp.where(low, swapped, zero), jnp.where(low, zero, x)], axis=0).astype(BF16)
        return carry

    lax.fori_loop(0, 4, step, 0)


def gather_kernel(x_ref, val_ref, ex, xc, vals, racc, cacc, rowx, colx, val_sem, send_sem, row_sem, col_sem):
    place = Place()
    loads = [pltpu.make_async_copy(val_ref.at[:, :, q], vals.at[:, q], val_sem.at[q]) for q in range(4)]
    for load in loads:
        load.start()
    place.greet()
    place.wait_greetings()
    out = Sender(send_sem)
    me_c, me_r = place.col, place.row
    out.send(x_ref, rowx.at[me_c], row_sem.at[me_c], place.y_lo)
    out.send(x_ref, colx.at[me_r], col_sem.at[me_r], place.y_hi)
    for to in place.xs:
        out.send(x_ref, rowx.at[me_c], row_sem.at[me_c], to)
    for to in place.zs:
        out.send(x_ref, colx.at[me_r], col_sem.at[me_r], to)
    out.send(x_ref, rowx.at[me_c], row_sem.at[me_c], place.sibling)
    expand_row(x_ref, ex, me_c)
    expand_col(x_ref, xc, me_r)

    def zero_rows(i, carry):
        racc[pl.ds(i * 16, 16)] = jnp.zeros((16, 16, 128), F32)
        return carry

    lax.fori_loop(0, NB_ROW // 16, zero_rows, 0)

    def zero_cols(i, carry):
        cacc[pl.ds(i * 16, 16)] = jnp.zeros((16, 8, 128), F32)
        return carry

    lax.fori_loop(0, NB_COL // 16, zero_cols, 0)

    def take_row(slot, targets):
        out.arrived(rowx.at[slot], row_sem.at[slot], place)
        for to in targets:
            out.send(rowx.at[slot], rowx.at[slot], row_sem.at[slot], to)
        expand_row(rowx.at[slot], ex, slot)

    def take_col(slot, targets):
        out.arrived(colx.at[slot], col_sem.at[slot], place)
        for to in targets:
            out.send(colx.at[slot], colx.at[slot], col_sem.at[slot], to)
        expand_col(colx.at[slot], xc, slot)

    yl, x, core, z, yh = place.yl, place.x, place.core, place.z, place.yh
    take_row(place.y_lo[1], place.xs + [place.sibling])
    take_col(place.y_hi[0], place.zs)
    for d in (1, 3, 2):
        take_row(place.col_of(yl, (x + d) % 4, core), [place.sibling])
        take_col(place.row_of((z + d) % 4, yh), [])
    for d in (1, 3, 2):
        take_row(place.col_of(1 - yl, (x + d) % 4, core), [place.sibling])
        take_col(place.row_of((z + d) % 4, 1 - yh), [])
    for d in (0, 1, 3, 2):
        take_row(place.col_of(yl, (x + d) % 4, 1 - core), [])
        take_row(place.col_of(1 - yl, (x + d) % 4, 1 - core), [])
    out.finish()
    for load in loads:
        load.wait()


def gather(basis_vectors, block_values):
    pairs = block_values.reshape(GROUPS, 4, 2, 32, 128).transpose(0, 3, 1, 2, 4)
    ex, xc, vals, racc, cacc = pl.pallas_call(
        gather_kernel,
        out_shape=(
            pltpu.VMEM((NB_ROW, 16, 128), BF16),
            pltpu.VMEM((NB_COL, 16, 128), BF16),
            pltpu.VMEM((GROUPS, 4, 32, 2, 128), BF16),
            pltpu.VMEM((NB_ROW + 1, 16, 128), F32),
            pltpu.VMEM((NB_COL + 1, 8, 128), F32),
        ),
        in_specs=[VMEM, ANY],
        out_specs=(VMEM,) * 5,
        scratch_shapes=[
            pltpu.VMEM((N_COL, NVEC, PIECE), BF16),
            pltpu.VMEM((N_ROW, NVEC, PIECE), BF16),
            pltpu.SemaphoreType.DMA((4,)),
            pltpu.SemaphoreType.DMA((23,)),
            pltpu.SemaphoreType.DMA((N_COL,)),
            pltpu.SemaphoreType.DMA((N_ROW,)),
        ],
        compiler_params=pltpu.CompilerParams(collective_id=0, has_side_effects=True, vmem_limit_bytes=8 * MIB),
    )(basis_vectors, pairs)
    return ex, xc, vals.reshape(GROUPS, 256, 128), racc, cacc


def product_kernel(count_ref, row_index, col_index, ex, xc, vals, racc_in, cacc_in, racc, cacc):
    count = count_ref[0]
    low, _ = lane_masks()
    lane = lax.broadcasted_iota(jnp.int32, (16, 128), 1)
    mine = [(lane // 64 == i // 2) & (lane % 2 == i % 2) for i in range(4)]
    weight = [jnp.where(m, 1.0, 0.0).astype(BF16) for m in mine]

    def group(t, guarded):
        base = t * 8
        rows = [row_index[base + s] for s in range(8)]
        cols = [col_index[base + s] for s in range(8)]
        to_rows, to_cols = rows, cols
        if guarded:
            to_rows = [jnp.where(base + s < count, rows[s], NB_ROW) for s in range(8)]
            to_cols = [jnp.where(base + s < count, cols[s], NB_COL) for s in range(8)]
        for h in range(2):
            a = vals[t, h * 128:(h + 1) * 128, :]
            left = jnp.concatenate([xc[cols[4 * h + i]] for i in range(4)], axis=0)
            right = jnp.concatenate([ex[rows[4 * h + i]] * weight[i] for i in range(4)], axis=0)
            forward = lax.dot_general(left, a, (((1,), (1,)), ((), ())), preferred_element_type=F32)
            backward = lax.dot_general(right, a, (((1,), (0,)), ((), ())), preferred_element_type=F32)
            for i in range(4):
                racc[to_rows[4 * h + i]] += jnp.where(mine[i], forward[i * 16:(i + 1) * 16], 0.0)
                cacc[to_cols[4 * h + i]] += jnp.where(low, backward[i * 16:i * 16 + 8], backward[i * 16 + 8:i * 16 + 16])

    whole = count // (8 * UNROLL)

    def fast(u, carry):
        for k in range(UNROLL):
            group(u * UNROLL + k, False)
        return carry

    lax.fori_loop(0, whole, fast, 0)

    def slow(t, carry):
        group(t, True)
        return carry

    lax.fori_loop(whole * UNROLL, (count + 7) // 8, slow, 0)


def products(count, row_index, col_index, ex, xc, vals, racc, cacc):
    return pl.pallas_call(
        product_kernel,
        out_shape=(pltpu.VMEM((NB_ROW + 1, 16, 128), F32), pltpu.VMEM((NB_COL + 1, 8, 128), F32)),
        in_specs=[SMEM, SMEM, SMEM, VMEM, VMEM, VMEM, VMEM, VMEM],
        out_specs=(VMEM, VMEM),
        input_output_aliases={6: 0, 7: 1},
        compiler_params=pltpu.CompilerParams(vmem_limit_bytes=4 * MIB),
    )(count, row_index, col_index, ex, xc, vals, racc, cacc)


def fold_row(racc, piece, put):
    low, even = lane_masks()

    def step(i, carry):
        for j in range(8):
            m = i * 8 + j
            ae, ao = racc[piece * 64 + 2 * m], racc[piece * 64 + 2 * m + 1]
            z = []
            for p in range(2):
                e, o = ae[p * 8:p * 8 + 8], ao[p * 8:p * 8 + 8]
                z.append(jnp.where(low, e, o) + pltpu.roll(jnp.where(low, o, e), 64, 1))
            w = jnp.where(even, z[1], z[0])
            y = jnp.where(even, z[0], z[1]) + jnp.where(even, pltpu.roll(w, 127, 1), pltpu.roll(w, 1, 1))
            put(pl.ds(pl.multiple_of(m * 128, 128), 128), y)
        return carry

    lax.fori_loop(0, 4, step, 0)


def fold_col(cacc, piece, put):
    low, _ = lane_masks()

    def step(i, carry):
        for j in range(8):
            m = i * 8 + j
            e, o = cacc[piece * 64 + 2 * m], cacc[piece * 64 + 2 * m + 1]
            put(pl.ds(pl.multiple_of(m * 128, 128), 128), jnp.where(low, e, o) + pltpu.roll(jnp.where(low, o, e), 64, 1))
        return carry

    lax.fori_loop(0, 4, step, 0)


def add_up(dst, terms):
    def step(i, carry):
        at = pl.ds(pl.multiple_of(i * 512, 512), 512)
        total = terms[0][:, at]
        for term in terms[1:]:
            total = total + term[:, at]
        dst[:, at] = total
        return carry

    lax.fori_loop(0, PIECE // 512, step, 0)


def scatter_kernel(racc, cacc, out_ref, for_core, from_core, row_part, from_x, row_sum, from_ylo,
                   col_part, from_z, col_sum, from_yhi, send_sem, core_sem, x_sem, ylo_sem, z_sem, yhi_sem):
    place = Place()
    place.greet()
    yl, x, core, z, yh = place.yl, place.x, place.core, place.z, place.yh
    out = Sender(send_sem)

    def write(ref):
        def put(at, y):
            ref[:, at] = y
        return put

    first = True
    for d in (1, 3, 2):
        for h in (1, 0):
            hh = 1 - yh if h else yh
            fold_col(cacc, place.row_of((z + d) % 4, hh), write(col_part.at[d, h]))
            if first:
                place.wait_greetings()
                first = False
            out.send(col_part.at[d, h], from_z.at[d - 1, h], z_sem.at[d - 1, h], place.zs[d - 1])
    for d in (1, 3, 2, 0):
        for h in (1, 0):
            hh = 1 - yl if h else yl
            fold_row(racc, place.col_of(hh, (x + d) % 4, 1 - core), write(for_core.at[d, h]))
            out.send(for_core.at[d, h], from_core.at[d, h], core_sem.at[d, h], place.sibling)
    for h in (1, 0):
        hh = 1 - yh if h else yh
        fold_col(cacc, place.row_of(z, hh), write(col_part.at[0, h]))
    for d in (1, 3, 2, 0):
        for h in (1, 0):
            hh = 1 - yl if h else yl
            out.arrived(from_core.at[d, h], core_sem.at[d, h], place)

            def put(at, y, d=d, h=h):
                row_part[d, h, :, at] = y + from_core[d, h, :, at]

            fold_row(racc, place.col_of(hh, (x + d) % 4, core), put)
            if d:
                out.send(row_part.at[d, h], from_x.at[d - 1, h], x_sem.at[d - 1, h], place.xs[d - 1])
    for d in (1, 3, 2):
        out.arrived(from_z.at[d - 1, 1], z_sem.at[d - 1, 1], place)
    add_up(col_sum.at[1], [col_part.at[0, 1]] + [from_z.at[k, 1] for k in range(3)])
    out.send(col_sum.at[1], from_yhi, yhi_sem.at[0], place.y_hi)
    for d in (1, 3, 2):
        out.arrived(from_x.at[d - 1, 1], x_sem.at[d - 1, 1], place)
    add_up(row_sum.at[1], [row_part.at[0, 1]] + [from_x.at[k, 1] for k in range(3)])
    out.send(row_sum.at[1], from_ylo, ylo_sem.at[0], place.y_lo)
    for d in (1, 3, 2):
        out.arrived(from_z.at[d - 1, 0], z_sem.at[d - 1, 0], place)
        out.arrived(from_x.at[d - 1, 0], x_sem.at[d - 1, 0], place)
    add_up(row_sum.at[0], [row_part.at[0, 0], col_part.at[0, 0]] + [from_x.at[k, 0] for k in range(3)] + [from_z.at[k, 0] for k in range(3)])
    out.arrived(from_yhi, yhi_sem.at[0], place)
    out.arrived(from_ylo, ylo_sem.at[0], place)
    add_up(out_ref, [row_sum.at[0], from_yhi, from_ylo])
    out.finish()


def scatter(racc, cacc):
    piece = (NVEC, PIECE)
    return pl.pallas_call(
        scatter_kernel,
        out_shape=jax.ShapeDtypeStruct(piece, F32),
        in_specs=[VMEM, VMEM],
        out_specs=VMEM,
        scratch_shapes=[
            pltpu.VMEM((4, 2) + piece, F32), pltpu.VMEM((4, 2) + piece, F32),
            pltpu.VMEM((4, 2) + piece, F32), pltpu.VMEM((3, 2) + piece, F32),
            pltpu.VMEM((2,) + piece, F32), pltpu.VMEM(piece, F32),
            pltpu.VMEM((4, 2) + piece, F32), pltpu.VMEM((3, 2) + piece, F32),
            pltpu.VMEM((2,) + piece, F32), pltpu.VMEM(piece, F32),
            pltpu.SemaphoreType.DMA((22,)),
            pltpu.SemaphoreType.DMA((4, 2)), pltpu.SemaphoreType.DMA((3, 2)), pltpu.SemaphoreType.DMA((1,)),
            pltpu.SemaphoreType.DMA((3, 2)), pltpu.SemaphoreType.DMA((1,)),
        ],
        compiler_params=pltpu.CompilerParams(collective_id=1, has_side_effects=True, vmem_limit_bytes=8 * MIB),
    )(racc, cacc)


def body(basis_vectors, block_values, blk_row, blk_col, block_count):
    ex, xc, vals, racc, cacc = gather(basis_vectors, block_values.reshape(CAP, BLK * BLK))
    racc, cacc = products(block_count.reshape(1), blk_row.reshape(CAP), blk_col.reshape(CAP), ex, xc, vals, racc, cacc)
    return scatter(racc, cacc)


def solution(mesh):
    return jax.shard_map(
        body,
        mesh=mesh,
        in_specs=(
            P(None, ("row", "col")),
            P("row", "col", None, None),
            P("row", "col", None),
            P("row", "col", None),
            P("row", "col"),
        ),
        out_specs=P(None, ("row", "col")),
        check_vma=False,
    )
```

```python
import jax
import jax.numpy as jnp
from jax import lax
from jax.experimental import pallas as pl
from jax.experimental.pallas import tpu as pltpu
from jax.sharding import PartitionSpec as P

BLK = 64
NVEC = 8
PIECE = 4096
CAP = 2048
N_ROW = 8
N_COL = 16
NB_ROW = 1024
NB_COL = 512
GROUPS = CAP // 8
UNROLL = 32
TOP = 32767.0
F32, BF16, I16, I32 = jnp.float32, jnp.bfloat16, jnp.int16, jnp.int32
MESH = pl.DeviceIdType.MESH
SMEM = pl.BlockSpec(memory_space=pltpu.SMEM)
VMEM = pl.BlockSpec(memory_space=pltpu.VMEM)
ANY = pl.BlockSpec(memory_space=pl.ANY)
MIB = 2**20


def lane_masks():
    lane = lax.broadcasted_iota(jnp.int32, (8, 128), 1)
    return lane < 64, lane % 2 == 0


class Place:
    def __init__(self):
        self.row, self.col = lax.axis_index("row"), lax.axis_index("col")
        self.z, self.yh = self.row // 2, self.row % 2
        self.yl, self.x, self.core = self.col // 8, (self.col // 2) % 4, self.col % 2
        self.sibling = (self.row, self.col_of(self.yl, self.x, 1 - self.core))
        self.y_lo = (self.row, self.col_of(1 - self.yl, self.x, self.core))
        self.y_hi = (self.row_of(self.z, 1 - self.yh), self.col)
        self.xs = [(self.row, self.col_of(self.yl, (self.x + d) % 4, self.core)) for d in (1, 2, 3)]
        self.zs = [(self.row_of((self.z + d) % 4, self.yh), self.col) for d in (1, 2, 3)]
        self.partners = [self.sibling, self.y_lo, self.y_hi] + self.xs + self.zs

    def col_of(self, yl, x, core):
        return (yl * 4 + x) * 2 + core

    def row_of(self, z, yh):
        return z * 2 + yh

    def greet(self):
        barrier = pltpu.get_barrier_semaphore()
        for partner in self.partners:
            pl.semaphore_signal(barrier, inc=1, device_id=partner, device_id_type=MESH)

    def wait_greetings(self):
        pl.semaphore_wait(pltpu.get_barrier_semaphore(), len(self.partners))


class Sender:
    def __init__(self, sems):
        self.sems, self.sent = sems, []

    def send(self, src, dst, recv_sem, to):
        copy = pltpu.make_async_remote_copy(
            src_ref=src, dst_ref=dst, send_sem=self.sems.at[len(self.sent)], recv_sem=recv_sem,
            device_id=to, device_id_type=MESH)
        copy.start()
        self.sent.append(copy)

    def arrived(self, dst, recv_sem, place):
        pltpu.make_async_remote_copy(
            src_ref=dst, dst_ref=dst, send_sem=self.sems.at[0], recv_sem=recv_sem,
            device_id=place.sibling, device_id_type=MESH).wait_recv()

    def finish(self):
        for copy in self.sent:
            copy.wait_send()


def block_rows(block):
    return pl.ds(pl.multiple_of(block * 8, 8), 8)


def lane_tile(m):
    return pl.ds(pl.multiple_of(m * 128, 128), 128)


def expand(src, dst, piece):
    low, _ = lane_masks()

    def step(i, carry):
        for j in range(16):
            m = i * 16 + j
            x = src[:, lane_tile(m)].astype(F32)
            swapped = pltpu.roll(x, 64, 1)
            dst[block_rows(piece * 64 + 2 * m), :] = jnp.where(low, x, swapped)
            dst[block_rows(piece * 64 + 2 * m + 1), :] = jnp.where(low, swapped, x)
        return carry

    lax.fori_loop(0, 2, step, 0)


def gather_kernel(count_ref, row_index, col_index, x_ref, val_ref, ex, xc, vals, racc, cacc, to_rows, to_cols, rowx, colx, val_sem, send_sem, row_sem, col_sem):
    place = Place()
    loads = [pltpu.make_async_copy(val_ref.at[:, :, q], vals.at[:, q], val_sem.at[q]) for q in range(4)]
    for load in loads:
        load.start()
    place.greet()
    place.wait_greetings()
    out = Sender(send_sem)
    me_c, me_r = place.col, place.row
    out.send(x_ref, rowx.at[me_c], row_sem.at[me_c], place.y_lo)
    out.send(x_ref, colx.at[me_r], col_sem.at[me_r], place.y_hi)
    for to in place.xs:
        out.send(x_ref, rowx.at[me_c], row_sem.at[me_c], to)
    for to in place.zs:
        out.send(x_ref, colx.at[me_r], col_sem.at[me_r], to)
    out.send(x_ref, rowx.at[me_c], row_sem.at[me_c], place.sibling)
    expand(x_ref, ex, me_c)
    expand(x_ref, xc, me_r)
    slot = lax.broadcasted_iota(I32, (16, 128), 0) * 128 + lax.broadcasted_iota(I32, (16, 128), 1)
    used = slot < count_ref[0]
    to_rows[...] = jnp.where(used, row_index[...], NB_ROW) * 8
    to_cols[...] = jnp.where(used, col_index[...], NB_COL) * 8
    spare = jnp.zeros((8, 128), F32)
    ex[block_rows(NB_ROW), :] = spare
    xc[block_rows(NB_COL), :] = spare

    def zero_rows(i, carry):
        at = pl.ds(pl.multiple_of(i * 128, 128), 128)
        racc[:, at, :] = jnp.zeros((2, 128, 128), F32)
        return carry

    lax.fori_loop(0, NB_ROW * 8 // 128, zero_rows, 0)

    def zero_cols(i, carry):
        cacc[pl.ds(pl.multiple_of(i * 128, 128), 128), :] = jnp.zeros((128, 128), F32)
        return carry

    lax.fori_loop(0, NB_COL * 8 // 128, zero_cols, 0)

    def take_row(slot, targets):
        out.arrived(rowx.at[slot], row_sem.at[slot], place)
        for to in targets:
            out.send(rowx.at[slot], rowx.at[slot], row_sem.at[slot], to)
        expand(rowx.at[slot], ex, slot)

    def take_col(slot, targets):
        out.arrived(colx.at[slot], col_sem.at[slot], place)
        for to in targets:
            out.send(colx.at[slot], colx.at[slot], col_sem.at[slot], to)
        expand(colx.at[slot], xc, slot)

    yl, x, core, z, yh = place.yl, place.x, place.core, place.z, place.yh
    take_row(place.y_lo[1], place.xs + [place.sibling])
    take_col(place.y_hi[0], place.zs)
    for d in (1, 3, 2):
        take_row(place.col_of(yl, (x + d) % 4, core), [place.sibling])
        take_col(place.row_of((z + d) % 4, yh), [])
    for d in (1, 3, 2):
        take_row(place.col_of(1 - yl, (x + d) % 4, core), [place.sibling])
        take_col(place.row_of((z + d) % 4, 1 - yh), [])
    for d in (0, 1, 3, 2):
        take_row(place.col_of(yl, (x + d) % 4, 1 - core), [])
        take_row(place.col_of(1 - yl, (x + d) % 4, 1 - core), [])
    out.finish()
    for load in loads:
        load.wait()


def gather(count, row_index, col_index, basis_vectors, block_values):
    pairs = block_values.reshape(GROUPS, 4, 2, 32, 128).transpose(0, 3, 1, 2, 4)
    ex, xc, vals, racc, cacc, to_rows, to_cols = pl.pallas_call(
        gather_kernel,
        out_shape=(
            pltpu.VMEM(((NB_ROW + 1) * 8, 128), F32),
            pltpu.VMEM(((NB_COL + 1) * 8, 128), F32),
            pltpu.VMEM((GROUPS, 4, 32, 2, 128), BF16),
            pltpu.VMEM((2, (NB_ROW + 1) * 8, 128), F32),
            pltpu.VMEM(((NB_COL + 1) * 8, 128), F32),
            pltpu.VMEM((16, 128), I32),
            pltpu.VMEM((16, 128), I32),
        ),
        in_specs=[SMEM, VMEM, VMEM, VMEM, ANY],
        out_specs=(VMEM,) * 7,
        scratch_shapes=[
            pltpu.VMEM((N_COL, NVEC, PIECE), BF16),
            pltpu.VMEM((N_ROW, NVEC, PIECE), BF16),
            pltpu.SemaphoreType.DMA((4,)),
            pltpu.SemaphoreType.DMA((23,)),
            pltpu.SemaphoreType.DMA((N_COL,)),
            pltpu.SemaphoreType.DMA((N_ROW,)),
        ],
        compiler_params=pltpu.CompilerParams(collective_id=0, has_side_effects=True, vmem_limit_bytes=8 * MIB),
    )(count, row_index, col_index, basis_vectors, pairs)
    return to_rows.reshape(CAP), to_cols.reshape(CAP), ex, xc, vals.reshape(GROUPS, 256, 128), racc, cacc


def product_kernel(count_ref, row_at, col_at, ex, xc, vals, racc_in, cacc_in, racc, cacc):
    low, _ = lane_masks()
    lane = lax.broadcasted_iota(I32, (8, 128), 1)
    mine = [(lane // 64 == i // 2) & (lane % 2 == i % 2) for i in range(4)]
    zero = jnp.zeros((8, 128), F32)

    def rows8(ref, s):
        return pl.ds(pl.multiple_of(ref[s], 8), 8)

    def operands(s, i):
        x = xc[rows8(col_at, s), :]
        left = jnp.concatenate([jnp.where(low, x, zero), jnp.where(low, zero, x)], axis=0).astype(BF16)
        x = ex[rows8(row_at, s), :]
        other = pltpu.roll(x, 1 if i % 2 else 127, 1)
        p0, p1 = (other, x) if i % 2 else (x, other)
        right = jnp.concatenate([jnp.where(mine[i], p0, zero), jnp.where(mine[i], p1, zero)], axis=0).astype(BF16)
        return left, right

    def group(t):
        pairs = [operands(t * 8 + s, s % 4) for s in range(8)]
        left = jnp.concatenate([p[0] for p in pairs], axis=0)
        right = jnp.concatenate([p[1] for p in pairs], axis=0)
        a = vals[t]
        forward = lax.dot_general(left, a, (((1,), (1,)), ((), ())), preferred_element_type=F32)
        wide = jnp.concatenate([a[:128], a[128:]], axis=1)
        backward = lax.dot_general(right, wide, (((1,), (0,)), ((), ())), preferred_element_type=F32)
        for s in range(8):
            to_row, to_col = rows8(row_at, t * 8 + s), rows8(col_at, t * 8 + s)
            h, i, m = s // 4 * 128, s * 16, mine[s % 4]
            racc[0, to_row, :] += jnp.where(m, forward[i:i + 8, h:h + 128], zero)
            racc[1, to_row, :] += jnp.where(m, forward[i + 8:i + 16, h:h + 128], zero)
            cacc[to_col, :] += jnp.where(low, backward[i:i + 8, h:h + 128], backward[i + 8:i + 16, h:h + 128])

    def step(u, carry):
        for k in range(UNROLL):
            group(u * UNROLL + k)
        return carry

    lax.fori_loop(0, (count_ref[0] + 8 * UNROLL - 1) // (8 * UNROLL), step, 0)


def products(count, row_at, col_at, ex, xc, vals, racc, cacc):
    return pl.pallas_call(
        product_kernel,
        out_shape=(pltpu.VMEM(racc.shape, F32), pltpu.VMEM(cacc.shape, F32)),
        in_specs=[SMEM, SMEM, SMEM, VMEM, VMEM, VMEM, VMEM, VMEM],
        out_specs=(VMEM, VMEM),
        input_output_aliases={6: 0, 7: 1},
        compiler_params=pltpu.CompilerParams(vmem_limit_bytes=4 * MIB),
    )(count, row_at, col_at, ex, xc, vals, racc, cacc)


def fold_row(racc, piece, put):
    low, even = lane_masks()

    def step(i, top):
        for j in range(16):
            m = i * 16 + j
            z = []
            for p in range(2):
                e, o = racc[p, block_rows(piece * 64 + 2 * m), :], racc[p, block_rows(piece * 64 + 2 * m + 1), :]
                z.append(jnp.where(low, e, o) + pltpu.roll(jnp.where(low, o, e), 64, 1))
            w = jnp.where(even, z[1], z[0])
            y = jnp.where(even, z[0], z[1]) + jnp.where(even, pltpu.roll(w, 127, 1), pltpu.roll(w, 1, 1))
            top = jnp.maximum(top, jnp.abs(put(lane_tile(m), y)))
        return top

    return lax.fori_loop(0, 2, step, jnp.zeros((8, 128), F32))


def fold_col(cacc, piece, put):
    low, _ = lane_masks()

    def step(i, top):
        for j in range(16):
            m = i * 16 + j
            e, o = cacc[block_rows(piece * 64 + 2 * m), :], cacc[block_rows(piece * 64 + 2 * m + 1), :]
            y = jnp.where(low, e, o) + pltpu.roll(jnp.where(low, o, e), 64, 1)
            top = jnp.maximum(top, jnp.abs(put(lane_tile(m), y)))
        return top

    return lax.fori_loop(0, 2, step, jnp.zeros((8, 128), F32))


def to_wire(src, top, data, scale):
    some = top > 1e-33
    inverse = jnp.where(some, TOP / jnp.where(some, top, 1.0), 0.0)
    scale[...] = top * (1.0 / TOP)

    def step(i, carry):
        for j in range(8):
            m = i * 8 + j
            halves = [jnp.round(src[:, lane_tile(m + 16 * k)] * inverse) for k in range(2)]
            data[:, lane_tile(m)] = jnp.concatenate(halves, axis=0).astype(I32).astype(I16)
        return carry

    lax.fori_loop(0, 2, step, 0)


def add_up(put, terms, wired):
    scales = [scale[...] for _, scale in wired]

    def step(i, top):
        for j in range(4):
            m = i * 4 + j
            arrived = [data[:, lane_tile(m)].astype(I32).astype(F32) for data, _ in wired]
            for k in range(2):
                at = lane_tile(m + 16 * k)
                total = None
                for term in terms:
                    total = term[:, at] if total is None else total + term[:, at]
                for a, scale in zip(arrived, scales):
                    total = total + a[8 * k:8 * k + 8] * scale
                put(at, total)
                top = jnp.maximum(top, jnp.abs(total))
        return top

    return lax.fori_loop(0, 4, step, jnp.zeros((8, 128), F32))


def scatter_kernel(racc, cacc, out_ref, for_core, from_core, row_part, col_part, sums,
                   out_data, out_scale, in_data, in_scale, send_sem, core_sem, data_sem, scale_sem):
    place = Place()
    place.greet()
    yl, x, core, z, yh = place.yl, place.x, place.core, place.z, place.yh
    out = Sender(send_sem)

    def write(ref):
        def put(at, y):
            ref[:, at] = y
            return y
        return put

    def ship(slot, src, top, to):
        to_wire(src, top, out_data.at[slot], out_scale.at[slot])
        out.send(out_scale.at[slot], in_scale.at[slot], scale_sem.at[slot], to)
        out.send(out_data.at[slot], in_data.at[slot], data_sem.at[slot], to)

    def receive(slot):
        out.arrived(in_scale.at[slot], scale_sem.at[slot], place)
        out.arrived(in_data.at[slot], data_sem.at[slot], place)
        return in_data.at[slot], in_scale.at[slot]

    for h in (1, 0):
        y_lo = 1 - yl if h else yl
        y_hi = 1 - yh if h else yh
        for d in (2, 1, 3, 0):
            fold_row(racc, place.col_of(y_lo, (x + d) % 4, 1 - core), write(for_core.at[d, h]))
            if h and d == 2:
                place.wait_greetings()
            out.send(for_core.at[d, h], from_core.at[d, h], core_sem.at[d, h], place.sibling)
        for d in (2, 1, 3, 0):
            top = fold_col(cacc, place.row_of((z + d) % 4, y_hi), write(col_part.at[d, h]))
            if d:
                ship(6 + (d - 1) * 2 + h, col_part.at[d, h], top, place.zs[d - 1])
        for d in (2, 1, 3, 0):
            out.arrived(from_core.at[d, h], core_sem.at[d, h], place)

            def put(at, y, d=d, h=h):
                y = y + from_core[d, h, :, at]
                row_part[d, h, :, at] = y
                return y

            top = fold_row(racc, place.col_of(y_lo, (x + d) % 4, core), put)
            if d:
                ship((d - 1) * 2 + h, row_part.at[d, h], top, place.xs[d - 1])
    wired = [receive(6 + (d - 1) * 2 + 1) for d in (1, 3, 2)]
    top = add_up(write(sums.at[1]), [col_part.at[0, 1]], wired)
    ship(13, sums.at[1], top, place.y_hi)
    wired = [receive((d - 1) * 2 + 1) for d in (1, 3, 2)]
    top = add_up(write(sums.at[0]), [row_part.at[0, 1]], wired)
    ship(12, sums.at[0], top, place.y_lo)
    wired = [receive(6 + (d - 1) * 2) for d in (1, 3, 2)] + [receive((d - 1) * 2) for d in (1, 3, 2)]
    add_up(write(sums.at[2]), [row_part.at[0, 0], col_part.at[0, 0]], wired)
    wired = [receive(13), receive(12)]
    add_up(write(out_ref), [sums.at[2]], wired)
    out.finish()


def scatter(racc, cacc):
    piece, wire, lanes = (NVEC, PIECE), (2 * NVEC, PIECE // 2), (NVEC, 128)
    return pl.pallas_call(
        scatter_kernel,
        out_shape=jax.ShapeDtypeStruct(piece, F32),
        in_specs=[VMEM, VMEM],
        out_specs=VMEM,
        scratch_shapes=[
            pltpu.VMEM((4, 2) + piece, F32), pltpu.VMEM((4, 2) + piece, F32),
            pltpu.VMEM((4, 2) + piece, F32), pltpu.VMEM((4, 2) + piece, F32), pltpu.VMEM((3,) + piece, F32),
            pltpu.VMEM((14,) + wire, I16), pltpu.VMEM((14,) + lanes, F32),
            pltpu.VMEM((14,) + wire, I16), pltpu.VMEM((14,) + lanes, F32),
            pltpu.SemaphoreType.DMA((36,)),
            pltpu.SemaphoreType.DMA((4, 2)), pltpu.SemaphoreType.DMA((14,)), pltpu.SemaphoreType.DMA((14,)),
        ],
        compiler_params=pltpu.CompilerParams(collective_id=1, has_side_effects=True, vmem_limit_bytes=8 * MIB),
    )(racc, cacc)


def body(basis_vectors, block_values, blk_row, blk_col, block_count):
    count = block_count.reshape(1)
    row_at, col_at, ex, xc, vals, racc, cacc = gather(
        count, blk_row.reshape(16, 128), blk_col.reshape(16, 128), basis_vectors, block_values.reshape(CAP, BLK * BLK))
    racc, cacc = products(count, row_at, col_at, ex, xc, vals, racc, cacc)
    return scatter(racc, cacc)


def solution(mesh):
    return jax.shard_map(
        body,
        mesh=mesh,
        in_specs=(
            P(None, ("row", "col")),
            P("row", "col", None, None),
            P("row", "col", None),
            P("row", "col", None),
            P("row", "col"),
        ),
        out_specs=P(None, ("row", "col")),
        check_vma=False,
    )
```

```python
import jax
import jax.numpy as jnp
from jax import lax
from jax.experimental import pallas as pl
from jax.experimental.pallas import tpu as pltpu
from jax.sharding import PartitionSpec as P

BLK = 64
NVEC = 8
PIECE = 4096
CAP = 2048
N_ROW = 8
N_COL = 16
NB_ROW = 1024
NB_COL = 512
GROUPS = CAP // 8
UNROLL = 64
TOP = 32767.0
F32, BF16, I16, I32 = jnp.float32, jnp.bfloat16, jnp.int16, jnp.int32
MESH = pl.DeviceIdType.MESH
SMEM = pl.BlockSpec(memory_space=pltpu.SMEM)
VMEM = pl.BlockSpec(memory_space=pltpu.VMEM)
ANY = pl.BlockSpec(memory_space=pl.ANY)
MIB = 2**20


def lane_masks():
    lane = lax.broadcasted_iota(jnp.int32, (8, 128), 1)
    return lane < 64, lane % 2 == 0


class Place:
    def __init__(self):
        self.row, self.col = lax.axis_index("row"), lax.axis_index("col")
        self.z, self.yh = self.row // 2, self.row % 2
        self.yl, self.x, self.core = self.col // 8, (self.col // 2) % 4, self.col % 2
        self.sibling = (self.row, self.col_of(self.yl, self.x, 1 - self.core))
        self.y_lo = (self.row, self.col_of(1 - self.yl, self.x, self.core))
        self.y_hi = (self.row_of(self.z, 1 - self.yh), self.col)
        self.xs = [(self.row, self.col_of(self.yl, (self.x + d) % 4, self.core)) for d in (1, 2, 3)]
        self.zs = [(self.row_of((self.z + d) % 4, self.yh), self.col) for d in (1, 2, 3)]
        self.partners = [self.sibling, self.y_lo, self.y_hi] + self.xs + self.zs

    def col_of(self, yl, x, core):
        return (yl * 4 + x) * 2 + core

    def row_of(self, z, yh):
        return z * 2 + yh

    def greet(self):
        barrier = pltpu.get_barrier_semaphore()
        for partner in self.partners:
            pl.semaphore_signal(barrier, inc=1, device_id=partner, device_id_type=MESH)

    def wait_greetings(self):
        pl.semaphore_wait(pltpu.get_barrier_semaphore(), len(self.partners))


class Sender:
    def __init__(self, sems):
        self.sems, self.sent = sems, []

    def send(self, src, dst, recv_sem, to):
        copy = pltpu.make_async_remote_copy(
            src_ref=src, dst_ref=dst, send_sem=self.sems.at[len(self.sent)], recv_sem=recv_sem,
            device_id=to, device_id_type=MESH)
        copy.start()
        self.sent.append(copy)

    def arrived(self, dst, recv_sem, place):
        pltpu.make_async_remote_copy(
            src_ref=dst, dst_ref=dst, send_sem=self.sems.at[0], recv_sem=recv_sem,
            device_id=place.sibling, device_id_type=MESH).wait_recv()

    def finish(self):
        for copy in self.sent:
            copy.wait_send()


def block_rows(block):
    return pl.ds(pl.multiple_of(block * 8, 8), 8)


def lane_tile(m):
    return pl.ds(pl.multiple_of(m * 128, 128), 128)


def expand(src, dst, piece):
    low, _ = lane_masks()

    def step(i, carry):
        for j in range(16):
            m = i * 16 + j
            x = src[:, lane_tile(m)].astype(F32)
            swapped = pltpu.roll(x, 64, 1)
            dst[block_rows(piece * 64 + 2 * m), :] = jnp.where(low, x, swapped)
            dst[block_rows(piece * 64 + 2 * m + 1), :] = jnp.where(low, swapped, x)
        return carry

    lax.fori_loop(0, 2, step, 0)


def gather_kernel(count_ref, row_in, col_in, x_in, val_ref, ex, xc, vals, racc, cacc, to_rows, to_cols,
                  x_ref, row_index, col_index, rowx, colx, in_sem, val_sem, send_sem, row_sem, col_sem):
    place = Place()
    small = [pltpu.make_async_copy(src, dst, in_sem.at[i]) for i, (src, dst) in enumerate(
        [(x_in, x_ref), (row_in, row_index), (col_in, col_index)])]
    for copy in small:
        copy.start()
    loads = [pltpu.make_async_copy(val_ref.at[:, :, q], vals.at[:, q], val_sem.at[q]) for q in range(4)]
    for load in loads:
        load.start()
    place.greet()
    for copy in small:
        copy.wait()
    place.wait_greetings()
    out = Sender(send_sem)
    me_c, me_r = place.col, place.row
    out.send(x_ref, rowx.at[me_c], row_sem.at[me_c], place.y_lo)
    out.send(x_ref, colx.at[me_r], col_sem.at[me_r], place.y_hi)
    for to in place.xs:
        out.send(x_ref, rowx.at[me_c], row_sem.at[me_c], to)
    for to in place.zs:
        out.send(x_ref, colx.at[me_r], col_sem.at[me_r], to)
    out.send(x_ref, rowx.at[me_c], row_sem.at[me_c], place.sibling)
    expand(x_ref, ex, me_c)
    expand(x_ref, xc, me_r)
    slot = lax.broadcasted_iota(I32, (16, 128), 0) * 128 + lax.broadcasted_iota(I32, (16, 128), 1)
    used = slot < count_ref[0]
    to_rows[...] = jnp.where(used, row_index[...], NB_ROW) * 8
    to_cols[...] = jnp.where(used, col_index[...], NB_COL) * 8
    spare = jnp.zeros((8, 128), F32)
    ex[block_rows(NB_ROW), :] = spare
    xc[block_rows(NB_COL), :] = spare

    def clear(acc, blocks):
        def step(i, carry):
            acc[pl.ds(pl.multiple_of(i * 256, 256), 256), :] = jnp.zeros((256, 128), F32)
            return carry

        lax.fori_loop(0, blocks * 8 // 256, step, 0)

    clear(racc, NB_ROW)
    clear(cacc, NB_COL)

    def take_row(slot, targets):
        out.arrived(rowx.at[slot], row_sem.at[slot], place)
        for to in targets:
            out.send(rowx.at[slot], rowx.at[slot], row_sem.at[slot], to)
        expand(rowx.at[slot], ex, slot)

    def take_col(slot, targets):
        out.arrived(colx.at[slot], col_sem.at[slot], place)
        for to in targets:
            out.send(colx.at[slot], colx.at[slot], col_sem.at[slot], to)
        expand(colx.at[slot], xc, slot)

    yl, x, core, z, yh = place.yl, place.x, place.core, place.z, place.yh
    take_row(place.y_lo[1], place.xs + [place.sibling])
    take_col(place.y_hi[0], place.zs)
    for d in (1, 3, 2):
        take_row(place.col_of(yl, (x + d) % 4, core), [place.sibling])
        take_col(place.row_of((z + d) % 4, yh), [])
    for d in (1, 3, 2):
        take_row(place.col_of(1 - yl, (x + d) % 4, core), [place.sibling])
        take_col(place.row_of((z + d) % 4, 1 - yh), [])
    for d in (0, 1, 3, 2):
        take_row(place.col_of(yl, (x + d) % 4, 1 - core), [])
        take_row(place.col_of(1 - yl, (x + d) % 4, 1 - core), [])
    out.finish()
    for load in loads:
        load.wait()


def gather(count, row_index, col_index, basis_vectors, block_values):
    pairs = block_values.reshape(GROUPS, 4, 2, 32, 128).transpose(0, 3, 1, 2, 4)
    ex, xc, vals, racc, cacc, to_rows, to_cols = pl.pallas_call(
        gather_kernel,
        out_shape=(
            pltpu.VMEM(((NB_ROW + 1) * 8, 128), F32),
            pltpu.VMEM(((NB_COL + 1) * 8, 128), F32),
            pltpu.VMEM((GROUPS, 4, 32, 2, 128), BF16),
            pltpu.VMEM(((NB_ROW + 1) * 8, 128), F32),
            pltpu.VMEM(((NB_COL + 1) * 8, 128), F32),
            pltpu.VMEM((16, 128), I32),
            pltpu.VMEM((16, 128), I32),
        ),
        in_specs=[SMEM, ANY, ANY, ANY, ANY],
        out_specs=(VMEM,) * 7,
        scratch_shapes=[
            pltpu.VMEM((NVEC, PIECE), BF16),
            pltpu.VMEM((16, 128), I32),
            pltpu.VMEM((16, 128), I32),
            pltpu.VMEM((N_COL, NVEC, PIECE), BF16),
            pltpu.VMEM((N_ROW, NVEC, PIECE), BF16),
            pltpu.SemaphoreType.DMA((3,)),
            pltpu.SemaphoreType.DMA((4,)),
            pltpu.SemaphoreType.DMA((23,)),
            pltpu.SemaphoreType.DMA((N_COL,)),
            pltpu.SemaphoreType.DMA((N_ROW,)),
        ],
        compiler_params=pltpu.CompilerParams(collective_id=0, has_side_effects=True, vmem_limit_bytes=28 * MIB),
    )(count, row_index, col_index, basis_vectors, pairs)
    return to_rows.reshape(CAP), to_cols.reshape(CAP), ex, xc, vals.reshape(GROUPS, 256, 128), racc, cacc


def product_kernel(count_ref, row_at, col_at, ex, xc, vals, racc_in, cacc_in, racc, cacc):
    low, _ = lane_masks()
    lane = lax.broadcasted_iota(I32, (8, 128), 1)
    mine = [(lane // 64 == i // 2) & (lane % 2 == i % 2) for i in range(4)]
    half = [lane // 64 == i // 2 for i in range(4)]
    zero = jnp.zeros((8, 128), F32)

    def rows8(ref, s):
        return pl.ds(pl.multiple_of(ref[s], 8), 8)

    def operands(s, i):
        x = xc[rows8(col_at, s), :]
        left = jnp.concatenate([jnp.where(low, x, zero), jnp.where(low, zero, x)], axis=0).astype(BF16)
        x = ex[rows8(row_at, s), :]
        other = pltpu.roll(x, 1 if i % 2 else 127, 1)
        p0, p1 = (other, x) if i % 2 else (x, other)
        right = jnp.concatenate([jnp.where(mine[i], p0, zero), jnp.where(mine[i], p1, zero)], axis=0).astype(BF16)
        return left, right

    def group(t):
        pairs = [operands(t * 8 + s, s % 4) for s in range(8)]
        left = jnp.concatenate([p[0] for p in pairs], axis=0)
        right = jnp.concatenate([p[1] for p in pairs], axis=0)
        a = vals[t]
        forward = lax.dot_general(left, a, (((1,), (1,)), ((), ())), preferred_element_type=F32)
        wide = jnp.concatenate([a[:128], a[128:]], axis=1)
        backward = lax.dot_general(right, wide, (((1,), (0,)), ((), ())), preferred_element_type=F32)
        for s in range(8):
            to_row, to_col = rows8(row_at, t * 8 + s), rows8(col_at, t * 8 + s)
            h, i, par = s // 4 * 128, s * 16, s % 2
            same = forward[i + 8 * par:i + 8 * par + 8, h:h + 128]
            other = pltpu.roll(forward[i + 8 - 8 * par:i + 16 - 8 * par, h:h + 128], 127 if par else 1, 1)
            racc[to_row, :] += jnp.where(half[s % 4], jnp.where(mine[s % 4], same, other), zero)
            cacc[to_col, :] += jnp.where(low, backward[i:i + 8, h:h + 128], backward[i + 8:i + 16, h:h + 128])

    def step(u, carry):
        for k in range(UNROLL):
            group(u * UNROLL + k)
        return carry

    lax.fori_loop(0, (count_ref[0] + 8 * UNROLL - 1) // (8 * UNROLL), step, 0)


def products(count, row_at, col_at, ex, xc, vals, racc, cacc):
    return pl.pallas_call(
        product_kernel,
        out_shape=(pltpu.VMEM(racc.shape, F32), pltpu.VMEM(cacc.shape, F32)),
        in_specs=[SMEM, SMEM, SMEM, VMEM, VMEM, VMEM, VMEM, VMEM],
        out_specs=(VMEM, VMEM),
        input_output_aliases={6: 0, 7: 1},
        compiler_params=pltpu.CompilerParams(vmem_limit_bytes=4 * MIB),
    )(count, row_at, col_at, ex, xc, vals, racc, cacc)


def fold(acc, piece, put):
    low, _ = lane_masks()

    def step(i, top):
        for j in range(16):
            m = i * 16 + j
            e, o = acc[block_rows(piece * 64 + 2 * m), :], acc[block_rows(piece * 64 + 2 * m + 1), :]
            y = jnp.where(low, e, o) + pltpu.roll(jnp.where(low, o, e), 64, 1)
            top = jnp.maximum(top, jnp.abs(put(lane_tile(m), y)))
        return top

    return lax.fori_loop(0, 2, step, jnp.zeros((8, 128), F32))


def to_wire(src, top, data, scale):
    some = top > 1e-33
    inverse = jnp.where(some, TOP / jnp.where(some, top, 1.0), 0.0)
    scale[...] = top * (1.0 / TOP)

    def step(i, carry):
        for j in range(8):
            m = i * 8 + j
            halves = [jnp.round(src[:, lane_tile(m + 16 * k)] * inverse) for k in range(2)]
            data[:, lane_tile(m)] = jnp.concatenate(halves, axis=0).astype(I32).astype(I16)
        return carry

    lax.fori_loop(0, 2, step, 0)


def add_up(put, terms, wired):
    scales = [scale[...] for _, scale in wired]

    def step(i, top):
        for j in range(4):
            m = i * 4 + j
            arrived = [data[:, lane_tile(m)].astype(I32).astype(F32) for data, _ in wired]
            for k in range(2):
                at = lane_tile(m + 16 * k)
                total = None
                for term in terms:
                    total = term[:, at] if total is None else total + term[:, at]
                for a, scale in zip(arrived, scales):
                    total = total + a[8 * k:8 * k + 8] * scale
                put(at, total)
                top = jnp.maximum(top, jnp.abs(total))
        return top

    return lax.fori_loop(0, 4, step, jnp.zeros((8, 128), F32))


def scatter_kernel(racc, cacc, out_ref, for_core, from_core, row_part, col_part, sums,
                   out_data, out_scale, in_data, in_scale, send_sem, core_sem, data_sem, scale_sem):
    place = Place()
    place.greet()
    yl, x, core, z, yh = place.yl, place.x, place.core, place.z, place.yh
    out = Sender(send_sem)

    def write(ref):
        def put(at, y):
            ref[:, at] = y
            return y
        return put

    def ship(slot, src, top, to):
        to_wire(src, top, out_data.at[slot], out_scale.at[slot])
        out.send(out_scale.at[slot], in_scale.at[slot], scale_sem.at[slot], to)
        out.send(out_data.at[slot], in_data.at[slot], data_sem.at[slot], to)

    def receive(slot):
        out.arrived(in_scale.at[slot], scale_sem.at[slot], place)
        out.arrived(in_data.at[slot], data_sem.at[slot], place)
        return in_data.at[slot], in_scale.at[slot]

    def for_sibling(h, d):
        fold(racc, place.col_of(1 - yl if h else yl, (x + d) % 4, 1 - core), write(for_core.at[d, h]))

    def send_sibling(h, d):
        out.send(for_core.at[d, h], from_core.at[d, h], core_sem.at[d, h], place.sibling)

    def columns(h, d):
        top = fold(cacc, place.row_of((z + d) % 4, 1 - yh if h else yh), write(col_part.at[d, h]))
        if d:
            ship(6 + (d - 1) * 2 + h, col_part.at[d, h], top, place.zs[d - 1])

    def rows(h, d):
        out.arrived(from_core.at[d, h], core_sem.at[d, h], place)

        def put(at, y):
            y = y + from_core[d, h, :, at]
            row_part[d, h, :, at] = y
            return y

        top = fold(racc, place.col_of(1 - yl if h else yl, (x + d) % 4, core), put)
        if d:
            ship((d - 1) * 2 + h, row_part.at[d, h], top, place.xs[d - 1])

    order = [(1, 2), (1, 1), (1, 3), (0, 2), (0, 1), (0, 3), (1, 0), (0, 0)]
    for_sibling(*order[0])
    for_sibling(*order[1])
    place.wait_greetings()
    send_sibling(*order[0])
    send_sibling(*order[1])
    for k in range(8):
        columns(*order[k])
        if k + 2 < 8:
            for_sibling(*order[k + 2])
            send_sibling(*order[k + 2])
        rows(*order[k])
    wired = [receive(6 + (d - 1) * 2 + 1) for d in (1, 3, 2)]
    top = add_up(write(sums.at[1]), [col_part.at[0, 1]], wired)
    ship(13, sums.at[1], top, place.y_hi)
    wired = [receive((d - 1) * 2 + 1) for d in (1, 3, 2)]
    top = add_up(write(sums.at[0]), [row_part.at[0, 1]], wired)
    ship(12, sums.at[0], top, place.y_lo)
    wired = [receive(6 + (d - 1) * 2) for d in (1, 3, 2)] + [receive((d - 1) * 2) for d in (1, 3, 2)]
    add_up(write(sums.at[2]), [row_part.at[0, 0], col_part.at[0, 0]], wired)
    wired = [receive(13), receive(12)]
    add_up(write(out_ref), [sums.at[2]], wired)
    out.finish()


def scatter(racc, cacc):
    piece, wire, lanes = (NVEC, PIECE), (2 * NVEC, PIECE // 2), (NVEC, 128)
    return pl.pallas_call(
        scatter_kernel,
        out_shape=jax.ShapeDtypeStruct(piece, F32),
        in_specs=[VMEM, VMEM],
        out_specs=VMEM,
        scratch_shapes=[
            pltpu.VMEM((4, 2) + piece, F32), pltpu.VMEM((4, 2) + piece, F32),
            pltpu.VMEM((4, 2) + piece, F32), pltpu.VMEM((4, 2) + piece, F32), pltpu.VMEM((3,) + piece, F32),
            pltpu.VMEM((14,) + wire, I16), pltpu.VMEM((14,) + lanes, F32),
            pltpu.VMEM((14,) + wire, I16), pltpu.VMEM((14,) + lanes, F32),
            pltpu.SemaphoreType.DMA((36,)),
            pltpu.SemaphoreType.DMA((4, 2)), pltpu.SemaphoreType.DMA((14,)), pltpu.SemaphoreType.DMA((14,)),
        ],
        compiler_params=pltpu.CompilerParams(collective_id=1, has_side_effects=True, vmem_limit_bytes=8 * MIB),
    )(racc, cacc)


def body(basis_vectors, block_values, blk_row, blk_col, block_count):
    count = block_count.reshape(1)
    row_at, col_at, ex, xc, vals, racc, cacc = gather(
        count, blk_row.reshape(16, 128), blk_col.reshape(16, 128), basis_vectors, block_values.reshape(CAP, BLK * BLK))
    racc, cacc = products(count, row_at, col_at, ex, xc, vals, racc, cacc)
    return scatter(racc, cacc)


def solution(mesh):
    return jax.shard_map(
        body,
        mesh=mesh,
        in_specs=(
            P(None, ("row", "col")),
            P("row", "col", None, None),
            P("row", "col", None),
            P("row", "col", None),
            P("row", "col"),
        ),
        out_specs=P(None, ("row", "col")),
        check_vma=False,
    )
```

```python
import jax
import jax.numpy as jnp
from jax import lax
from jax.experimental import pallas as pl
from jax.experimental.pallas import tpu as pltpu
from jax.sharding import PartitionSpec as P

BLK = 64
NVEC = 8
PIECE = 4096
CAP = 2048
N_ROW = 8
N_COL = 16
NB_ROW = 1024
NB_COL = 512
GROUPS = CAP // 8
UNROLL = 64
TOP = 32767.0
F32, BF16, I16, I32 = jnp.float32, jnp.bfloat16, jnp.int16, jnp.int32
MESH = pl.DeviceIdType.MESH
SMEM = pl.BlockSpec(memory_space=pltpu.SMEM)
VMEM = pl.BlockSpec(memory_space=pltpu.VMEM)
ANY = pl.BlockSpec(memory_space=pl.ANY)
MIB = 2**20


def lane_masks():
    lane = lax.broadcasted_iota(jnp.int32, (8, 128), 1)
    return lane < 64, lane % 2 == 0


class Place:
    def __init__(self):
        self.row, self.col = lax.axis_index("row"), lax.axis_index("col")
        self.z, self.yh = self.row // 2, self.row % 2
        self.yl, self.x, self.core = self.col // 8, (self.col // 2) % 4, self.col % 2
        self.sibling = (self.row, self.col_of(self.yl, self.x, 1 - self.core))
        self.y_lo = (self.row, self.col_of(1 - self.yl, self.x, self.core))
        self.y_hi = (self.row_of(self.z, 1 - self.yh), self.col)
        self.xs = [(self.row, self.col_of(self.yl, (self.x + d) % 4, self.core)) for d in (1, 2, 3)]
        self.zs = [(self.row_of((self.z + d) % 4, self.yh), self.col) for d in (1, 2, 3)]
        self.partners = [self.sibling, self.y_lo, self.y_hi] + self.xs + self.zs

    def col_of(self, yl, x, core):
        return (yl * 4 + x) * 2 + core

    def row_of(self, z, yh):
        return z * 2 + yh

    def greet(self):
        barrier = pltpu.get_barrier_semaphore()
        for partner in self.partners:
            pl.semaphore_signal(barrier, inc=1, device_id=partner, device_id_type=MESH)

    def wait_greetings(self):
        pl.semaphore_wait(pltpu.get_barrier_semaphore(), len(self.partners))


class Sender:
    def __init__(self, sems):
        self.sems, self.sent = sems, []

    def send(self, src, dst, recv_sem, to):
        copy = pltpu.make_async_remote_copy(
            src_ref=src, dst_ref=dst, send_sem=self.sems.at[len(self.sent)], recv_sem=recv_sem,
            device_id=to, device_id_type=MESH)
        copy.start()
        self.sent.append(copy)

    def arrived(self, dst, recv_sem, place):
        pltpu.make_async_remote_copy(
            src_ref=dst, dst_ref=dst, send_sem=self.sems.at[0], recv_sem=recv_sem,
            device_id=place.sibling, device_id_type=MESH).wait_recv()

    def finish(self):
        for copy in self.sent:
            copy.wait_send()


def block_rows(block):
    return pl.ds(pl.multiple_of(block * 8, 8), 8)


def lane_tile(m):
    return pl.ds(pl.multiple_of(m * 128, 128), 128)


def expand(src, dst, piece):
    low, _ = lane_masks()

    def step(i, carry):
        for j in range(16):
            m = i * 16 + j
            x = src[:, lane_tile(m)].astype(F32)
            swapped = pltpu.roll(x, 64, 1)
            dst[block_rows(piece * 64 + 2 * m), :] = jnp.where(low, x, swapped)
            dst[block_rows(piece * 64 + 2 * m + 1), :] = jnp.where(low, swapped, x)
        return carry

    lax.fori_loop(0, 2, step, 0)


def gather_kernel(count_ref, row_in, col_in, x_in, val_ref, ex, xc, vals, racc, cacc, to_rows, to_cols,
                  row_index, col_index, rowx, colx, in_sem, val_sem, send_sem, row_sem, col_sem, core_sem):
    place = Place()
    yl, x, core, z, yh = place.yl, place.x, place.core, place.z, place.yh
    me_r = place.row

    def file(core, yl, x):
        return core * 8 + yl * 4 + x

    mine = file(core, yl, x)
    small = [pltpu.make_async_copy(src, dst, in_sem.at[i]) for i, (src, dst) in enumerate(
        [(x_in, rowx.at[mine]), (row_in, row_index), (col_in, col_index)])]
    for copy in small:
        copy.start()
    loads = [pltpu.make_async_copy(val_ref.at[:, :, q], vals.at[:, q], val_sem.at[q]) for q in range(4)]
    for load in loads:
        load.start()
    place.greet()
    for copy in small:
        copy.wait()
    place.wait_greetings()
    out = Sender(send_sem)
    own = rowx.at[mine]
    out.send(own, rowx.at[mine], row_sem.at[mine], place.y_lo)
    out.send(own, colx.at[me_r], col_sem.at[me_r], place.y_hi)
    for d in (0, 2, 1):
        out.send(own, rowx.at[mine], row_sem.at[mine], place.xs[d])
        out.send(own, colx.at[me_r], col_sem.at[me_r], place.zs[d])
    expand(own, ex, place.col)
    expand(own, xc, me_r)
    slot = lax.broadcasted_iota(I32, (16, 128), 0) * 128 + lax.broadcasted_iota(I32, (16, 128), 1)
    used = slot < count_ref[0]
    to_rows[...] = jnp.where(used, row_index[...], NB_ROW) * 8
    to_cols[...] = jnp.where(used, col_index[...], NB_COL) * 8
    spare = jnp.zeros((8, 128), F32)
    ex[block_rows(NB_ROW), :] = spare
    xc[block_rows(NB_COL), :] = spare

    def clear(acc, blocks):
        def step(i, carry):
            acc[pl.ds(pl.multiple_of(i * 256, 256), 256), :] = jnp.zeros((256, 128), F32)
            return carry

        lax.fori_loop(0, blocks * 8 // 256, step, 0)

    clear(racc, NB_ROW)
    clear(cacc, NB_COL)

    def take_row(y, d, targets):
        at = file(core, y, (x + d) % 4)
        out.arrived(rowx.at[at], row_sem.at[at], place)
        for to in targets:
            out.send(rowx.at[at], rowx.at[at], row_sem.at[at], to)

    def take_col(slot, targets):
        out.arrived(colx.at[slot], col_sem.at[slot], place)
        for to in targets:
            out.send(colx.at[slot], colx.at[slot], col_sem.at[slot], to)

    def four(c, y):
        return rowx.at[pl.ds(file(c, y, 0), 4)]

    def give(y):
        out.send(four(core, y), four(core, y), core_sem.at[y], place.sibling)

    def expand_row(c, y, d):
        expand(rowx.at[file(c, y, (x + d) % 4)], ex, place.col_of(y, (x + d) % 4, c))

    take_row(1 - yl, 0, [place.xs[0], place.xs[2], place.xs[1]])
    take_col(place.row_of(z, 1 - yh), [place.zs[0], place.zs[2], place.zs[1]])
    for d in (1, 3, 2):
        take_row(yl, d, [])
    give(yl)
    expand_row(core, 1 - yl, 0)
    expand(colx.at[place.row_of(z, 1 - yh)], xc, place.row_of(z, 1 - yh))
    for d in (1, 3, 2):
        expand_row(core, yl, d)
    for d in (1, 3, 2):
        take_col(place.row_of((z + d) % 4, yh), [])
        expand(colx.at[place.row_of((z + d) % 4, yh)], xc, place.row_of((z + d) % 4, yh))
    for d in (1, 3, 2):
        take_row(1 - yl, d, [])
    give(1 - yl)
    out.arrived(four(1 - core, yl), core_sem.at[yl], place)
    for d in (0, 1, 2, 3):
        expand_row(1 - core, yl, d)
    for d in (1, 3, 2):
        expand_row(core, 1 - yl, d)
    for d in (1, 3, 2):
        take_col(place.row_of((z + d) % 4, 1 - yh), [])
        expand(colx.at[place.row_of((z + d) % 4, 1 - yh)], xc, place.row_of((z + d) % 4, 1 - yh))
    out.arrived(four(1 - core, 1 - yl), core_sem.at[1 - yl], place)
    for d in (0, 1, 2, 3):
        expand_row(1 - core, 1 - yl, d)
    out.finish()
    for load in loads:
        load.wait()


def gather(count, row_index, col_index, basis_vectors, block_values):
    pairs = block_values.reshape(GROUPS, 4, 2, 32, 128).transpose(0, 3, 1, 2, 4)
    ex, xc, vals, racc, cacc, to_rows, to_cols = pl.pallas_call(
        gather_kernel,
        out_shape=(
            pltpu.VMEM(((NB_ROW + 1) * 8, 128), F32),
            pltpu.VMEM(((NB_COL + 1) * 8, 128), F32),
            pltpu.VMEM((GROUPS, 4, 32, 2, 128), BF16),
            pltpu.VMEM(((NB_ROW + 1) * 8, 128), F32),
            pltpu.VMEM(((NB_COL + 1) * 8, 128), F32),
            pltpu.VMEM((16, 128), I32),
            pltpu.VMEM((16, 128), I32),
        ),
        in_specs=[SMEM, ANY, ANY, ANY, ANY],
        out_specs=(VMEM,) * 7,
        scratch_shapes=[
            pltpu.VMEM((16, 128), I32),
            pltpu.VMEM((16, 128), I32),
            pltpu.VMEM((N_COL, NVEC, PIECE), BF16),
            pltpu.VMEM((N_ROW, NVEC, PIECE), BF16),
            pltpu.SemaphoreType.DMA((3,)),
            pltpu.SemaphoreType.DMA((4,)),
            pltpu.SemaphoreType.DMA((16,)),
            pltpu.SemaphoreType.DMA((N_COL,)),
            pltpu.SemaphoreType.DMA((N_ROW,)),
            pltpu.SemaphoreType.DMA((2,)),
        ],
        compiler_params=pltpu.CompilerParams(collective_id=0, has_side_effects=True, vmem_limit_bytes=28 * MIB),
    )(count, row_index, col_index, basis_vectors, pairs)
    return to_rows.reshape(CAP), to_cols.reshape(CAP), ex, xc, vals.reshape(GROUPS, 256, 128), racc, cacc


def product_kernel(count_ref, row_at, col_at, ex, xc, vals, racc_in, cacc_in, racc, cacc):
    low, _ = lane_masks()
    lane = lax.broadcasted_iota(I32, (8, 128), 1)
    mine = [(lane // 64 == i // 2) & (lane % 2 == i % 2) for i in range(4)]
    half = [lane // 64 == i // 2 for i in range(4)]
    zero = jnp.zeros((8, 128), F32)

    def rows8(ref, s):
        return pl.ds(pl.multiple_of(ref[s], 8), 8)

    def operands(s, i):
        x = xc[rows8(col_at, s), :]
        left = jnp.concatenate([jnp.where(low, x, zero), jnp.where(low, zero, x)], axis=0).astype(BF16)
        x = ex[rows8(row_at, s), :]
        other = pltpu.roll(x, 1 if i % 2 else 127, 1)
        p0, p1 = (other, x) if i % 2 else (x, other)
        right = jnp.concatenate([jnp.where(mine[i], p0, zero), jnp.where(mine[i], p1, zero)], axis=0).astype(BF16)
        return left, right

    def group(t):
        pairs = [operands(t * 8 + s, s % 4) for s in range(8)]
        left = jnp.concatenate([p[0] for p in pairs], axis=0)
        right = jnp.concatenate([p[1] for p in pairs], axis=0)
        a = vals[t]
        forward = lax.dot_general(left, a, (((1,), (1,)), ((), ())), preferred_element_type=F32)
        wide = jnp.concatenate([a[:128], a[128:]], axis=1)
        backward = lax.dot_general(right, wide, (((1,), (0,)), ((), ())), preferred_element_type=F32)
        for s in range(8):
            to_row, to_col = rows8(row_at, t * 8 + s), rows8(col_at, t * 8 + s)
            h, i, par = s // 4 * 128, s * 16, s % 2
            same = forward[i + 8 * par:i + 8 * par + 8, h:h + 128]
            other = pltpu.roll(forward[i + 8 - 8 * par:i + 16 - 8 * par, h:h + 128], 127 if par else 1, 1)
            racc[to_row, :] += jnp.where(half[s % 4], jnp.where(mine[s % 4], same, other), zero)
            cacc[to_col, :] += jnp.where(low, backward[i:i + 8, h:h + 128], backward[i + 8:i + 16, h:h + 128])

    def step(u, carry):
        for k in range(UNROLL):
            group(u * UNROLL + k)
        return carry

    lax.fori_loop(0, (count_ref[0] + 8 * UNROLL - 1) // (8 * UNROLL), step, 0)


def products(count, row_at, col_at, ex, xc, vals, racc, cacc):
    return pl.pallas_call(
        product_kernel,
        out_shape=(pltpu.VMEM(racc.shape, F32), pltpu.VMEM(cacc.shape, F32)),
        in_specs=[SMEM, SMEM, SMEM, VMEM, VMEM, VMEM, VMEM, VMEM],
        out_specs=(VMEM, VMEM),
        input_output_aliases={6: 0, 7: 1},
        compiler_params=pltpu.CompilerParams(vmem_limit_bytes=4 * MIB),
    )(count, row_at, col_at, ex, xc, vals, racc, cacc)


def fold(acc, piece, put):
    low, _ = lane_masks()

    def step(i, top):
        for j in range(16):
            m = i * 16 + j
            e, o = acc[block_rows(piece * 64 + 2 * m), :], acc[block_rows(piece * 64 + 2 * m + 1), :]
            y = jnp.where(low, e, o) + pltpu.roll(jnp.where(low, o, e), 64, 1)
            top = jnp.maximum(top, jnp.abs(put(lane_tile(m), y)))
        return top

    return lax.fori_loop(0, 2, step, jnp.zeros((8, 128), F32))


def scale_of(code):
    return jnp.exp2(code * (1.0 / 256.0))


def to_wire(src, top, wire):
    some = top > 1e-33
    code = jnp.ceil(jnp.log2(jnp.where(some, top, 1.0)) * 256.0) + 1.0
    inverse = jnp.where(some, TOP / scale_of(code), 0.0)
    wire[:, lane_tile(16)] = jnp.concatenate([code, code], axis=0).astype(I32).astype(I16)

    def step(i, carry):
        for j in range(8):
            m = i * 8 + j
            halves = [jnp.round(src[:, lane_tile(m + 16 * k)] * inverse) for k in range(2)]
            wire[:, lane_tile(m)] = jnp.concatenate(halves, axis=0).astype(I32).astype(I16)
        return carry

    lax.fori_loop(0, 2, step, 0)


def add_up(put, terms, wires):
    scales = [scale_of(wire[:, lane_tile(16)].astype(I32).astype(F32)[:8]) * (1.0 / TOP) for wire in wires]

    def step(i, top):
        for j in range(4):
            m = i * 4 + j
            arrived = [wire[:, lane_tile(m)].astype(I32).astype(F32) for wire in wires]
            for k in range(2):
                at = lane_tile(m + 16 * k)
                total = None
                for term in terms:
                    total = term[:, at] if total is None else total + term[:, at]
                for a, scale in zip(arrived, scales):
                    total = total + a[8 * k:8 * k + 8] * scale
                put(at, total)
                top = jnp.maximum(top, jnp.abs(total))
        return top

    return lax.fori_loop(0, 4, step, jnp.zeros((8, 128), F32))


def scatter_kernel(racc, cacc, out_ref, for_core, from_core, row_part, col_part, sums,
                   out_wire, in_wire, send_sem, core_sem, wire_sem):
    place = Place()
    place.greet()
    yl, x, core, z, yh = place.yl, place.x, place.core, place.z, place.yh
    out = Sender(send_sem)

    def write(ref):
        def put(at, y):
            ref[:, at] = y
            return y
        return put

    def ship(at, to):
        out.send(out_wire.at[at], in_wire.at[at], wire_sem.at[at], to)

    def receive(at):
        out.arrived(in_wire.at[at], wire_sem.at[at], place)

    order = [(1, 2), (1, 1), (1, 3), (0, 2), (0, 1), (0, 3), (1, 0), (0, 0)]

    def for_sibling(k):
        h, d = order[k]
        fold(racc, place.col_of(1 - yl if h else yl, (x + d) % 4, 1 - core), write(for_core.at[k]))

    def send_sibling(k):
        out.send(for_core.at[k], from_core.at[k], core_sem.at[k], place.sibling)

    def columns(k):
        h, d = order[k]
        at = 6 + (d - 1) * 2 + h
        top = fold(cacc, place.row_of((z + d) % 4, 1 - yh if h else yh), write(col_part.at[d, h]))
        if d:
            to_wire(col_part.at[d, h], top, out_wire.at[at])
            ship(at, place.zs[d - 1])

    def rows(k):
        h, d = order[k]
        out.arrived(from_core.at[k], core_sem.at[k], place)

        def put(at, y):
            y = y + from_core[k, :, at]
            row_part[d, h, :, at] = y
            return y

        top = fold(racc, place.col_of(1 - yl if h else yl, (x + d) % 4, core), put)
        if d:
            to_wire(row_part.at[d, h], top, out_wire.at[(d - 1) * 2 + h])
            ship((d - 1) * 2 + h, place.xs[d - 1])

    for_sibling(0)
    for_sibling(1)
    place.wait_greetings()
    send_sibling(0)
    send_sibling(1)
    for k in range(8):
        columns(k)
        if k + 2 < 8:
            for_sibling(k + 2)
            send_sibling(k + 2)
        rows(k)
    for d in (1, 3, 2):
        receive(6 + (d - 1) * 2 + 1)
    top = add_up(write(sums.at[1]), [col_part.at[0, 1]], [in_wire.at[6 + (d - 1) * 2 + 1] for d in (1, 3, 2)])
    to_wire(sums.at[1], top, out_wire.at[13])
    ship(13, place.y_hi)
    for d in (1, 3, 2):
        receive((d - 1) * 2 + 1)
    top = add_up(write(sums.at[0]), [row_part.at[0, 1]], [in_wire.at[(d - 1) * 2 + 1] for d in (1, 3, 2)])
    to_wire(sums.at[0], top, out_wire.at[12])
    ship(12, place.y_lo)
    for d in (1, 3, 2):
        receive((d - 1) * 2)
        receive(6 + (d - 1) * 2)
    add_up(write(sums.at[2]), [row_part.at[0, 0], col_part.at[0, 0]],
           [in_wire.at[(d - 1) * 2] for d in (1, 3, 2)] + [in_wire.at[6 + (d - 1) * 2] for d in (1, 3, 2)])
    receive(13)
    receive(12)
    add_up(write(out_ref), [sums.at[2]], [in_wire.at[13], in_wire.at[12]])
    out.finish()


def scatter(racc, cacc):
    piece, wire = (NVEC, PIECE), (2 * NVEC, PIECE // 2 + 128)
    return pl.pallas_call(
        scatter_kernel,
        out_shape=jax.ShapeDtypeStruct(piece, F32),
        in_specs=[VMEM, VMEM],
        out_specs=VMEM,
        scratch_shapes=[
            pltpu.VMEM((8,) + piece, F32), pltpu.VMEM((8,) + piece, F32),
            pltpu.VMEM((4, 2) + piece, F32), pltpu.VMEM((4, 2) + piece, F32), pltpu.VMEM((3,) + piece, F32),
            pltpu.VMEM((14,) + wire, I16), pltpu.VMEM((14,) + wire, I16),
            pltpu.SemaphoreType.DMA((22,)),
            pltpu.SemaphoreType.DMA((8,)), pltpu.SemaphoreType.DMA((14,)),
        ],
        compiler_params=pltpu.CompilerParams(collective_id=1, has_side_effects=True, vmem_limit_bytes=8 * MIB),
    )(racc, cacc)


def body(basis_vectors, block_values, blk_row, blk_col, block_count):
    count = block_count.reshape(1)
    row_at, col_at, ex, xc, vals, racc, cacc = gather(
        count, blk_row.reshape(16, 128), blk_col.reshape(16, 128), basis_vectors, block_values.reshape(CAP, BLK * BLK))
    racc, cacc = products(count, row_at, col_at, ex, xc, vals, racc, cacc)
    return scatter(racc, cacc)


def solution(mesh):
    return jax.shard_map(
        body,
        mesh=mesh,
        in_specs=(
            P(None, ("row", "col")),
            P("row", "col", None, None),
            P("row", "col", None),
            P("row", "col", None),
            P("row", "col"),
        ),
        out_specs=P(None, ("row", "col")),
        check_vma=False,
    )
```

```python
import jax
import jax.numpy as jnp
from jax import lax
from jax.experimental import pallas as pl
from jax.experimental.pallas import tpu as pltpu
from jax.sharding import PartitionSpec as P

BLK = 64
NVEC = 8
PIECE = 4096
CAP = 2048
N_ROW = 8
N_COL = 16
NB_ROW = 1024
NB_COL = 512
GROUPS = CAP // 8
UNROLL = 128
TOP = 32767.0
F32, BF16, I16, I32 = jnp.float32, jnp.bfloat16, jnp.int16, jnp.int32
MESH = pl.DeviceIdType.MESH
SMEM = pl.BlockSpec(memory_space=pltpu.SMEM)
VMEM = pl.BlockSpec(memory_space=pltpu.VMEM)
ANY = pl.BlockSpec(memory_space=pl.ANY)
MIB = 2**20


def lane_masks():
    lane = lax.broadcasted_iota(jnp.int32, (8, 128), 1)
    return lane < 64, lane % 2 == 0


class Place:
    def __init__(self):
        self.row, self.col = lax.axis_index("row"), lax.axis_index("col")
        self.z, self.yh = self.row // 2, self.row % 2
        self.yl, self.x, self.core = self.col // 8, (self.col // 2) % 4, self.col % 2
        self.sibling = (self.row, self.col_of(self.yl, self.x, 1 - self.core))
        self.y_lo = (self.row, self.col_of(1 - self.yl, self.x, self.core))
        self.y_hi = (self.row_of(self.z, 1 - self.yh), self.col)
        self.xs = [(self.row, self.col_of(self.yl, (self.x + d) % 4, self.core)) for d in (1, 2, 3)]
        self.zs = [(self.row_of((self.z + d) % 4, self.yh), self.col) for d in (1, 2, 3)]
        self.partners = [self.sibling, self.y_lo, self.y_hi] + self.xs + self.zs

    def col_of(self, yl, x, core):
        return (yl * 4 + x) * 2 + core

    def row_of(self, z, yh):
        return z * 2 + yh

    def greet(self):
        barrier = pltpu.get_barrier_semaphore()
        for partner in self.partners:
            pl.semaphore_signal(barrier, inc=1, device_id=partner, device_id_type=MESH)

    def wait_greetings(self):
        pl.semaphore_wait(pltpu.get_barrier_semaphore(), len(self.partners))


class Sender:
    def __init__(self, sems):
        self.sems, self.sent = sems, []

    def send(self, src, dst, recv_sem, to):
        copy = pltpu.make_async_remote_copy(
            src_ref=src, dst_ref=dst, send_sem=self.sems.at[len(self.sent)], recv_sem=recv_sem,
            device_id=to, device_id_type=MESH)
        copy.start()
        self.sent.append(copy)

    def arrived(self, dst, recv_sem, place):
        pltpu.make_async_remote_copy(
            src_ref=dst, dst_ref=dst, send_sem=self.sems.at[0], recv_sem=recv_sem,
            device_id=place.sibling, device_id_type=MESH).wait_recv()

    def finish(self):
        for copy in self.sent:
            copy.wait_send()


def block_rows(block):
    return pl.ds(pl.multiple_of(block * 8, 8), 8)


def lane_tile(m):
    return pl.ds(pl.multiple_of(m * 128, 128), 128)


def expand(src, dst, piece):
    low, _ = lane_masks()

    def step(i, carry):
        for j in range(16):
            m = i * 16 + j
            x = src[:, lane_tile(m)].astype(F32)
            swapped = pltpu.roll(x, 64, 1)
            dst[block_rows(piece * 64 + 2 * m), :] = jnp.where(low, x, swapped)
            dst[block_rows(piece * 64 + 2 * m + 1), :] = jnp.where(low, swapped, x)
        return carry

    lax.fori_loop(0, 2, step, 0)


def gather_kernel(count_ref, row_in, col_in, x_in, val_ref, ex, xc, vals, racc, cacc, to_rows, to_cols,
                  row_index, col_index, rowx, colx, in_sem, val_sem, send_sem, row_sem, col_sem, core_sem):
    place = Place()
    yl, x, core, z, yh = place.yl, place.x, place.core, place.z, place.yh
    me_r = place.row

    def file(core, yl, x):
        return core * 8 + yl * 4 + x

    mine = file(core, yl, x)
    small = [pltpu.make_async_copy(src, dst, in_sem.at[i]) for i, (src, dst) in enumerate(
        [(x_in, rowx.at[mine]), (row_in, row_index), (col_in, col_index)])]
    for copy in small:
        copy.start()
    loads = [pltpu.make_async_copy(val_ref.at[:, :, q], vals.at[:, q], val_sem.at[q]) for q in range(4)]
    for load in loads:
        load.start()
    place.greet()
    for copy in small:
        copy.wait()
    place.wait_greetings()
    out = Sender(send_sem)
    own = rowx.at[mine]
    out.send(own, rowx.at[mine], row_sem.at[mine], place.y_lo)
    out.send(own, colx.at[me_r], col_sem.at[me_r], place.y_hi)
    for d in (0, 2, 1):
        out.send(own, rowx.at[mine], row_sem.at[mine], place.xs[d])
        out.send(own, colx.at[me_r], col_sem.at[me_r], place.zs[d])
    expand(own, ex, place.col)
    expand(own, xc, me_r)
    slot = lax.broadcasted_iota(I32, (16, 128), 0) * 128 + lax.broadcasted_iota(I32, (16, 128), 1)
    used = slot < count_ref[0]
    to_rows[...] = jnp.where(used, row_index[...], NB_ROW) * 8
    to_cols[...] = jnp.where(used, col_index[...], NB_COL) * 8
    spare = jnp.zeros((8, 128), F32)
    ex[block_rows(NB_ROW), :] = spare
    xc[block_rows(NB_COL), :] = spare

    def clear(acc, blocks):
        def step(i, carry):
            acc[pl.ds(pl.multiple_of(i * 256, 256), 256), :] = jnp.zeros((256, 128), F32)
            return carry

        lax.fori_loop(0, blocks * 8 // 256, step, 0)

    clear(racc, NB_ROW)
    clear(cacc, NB_COL)

    def take_row(y, d, targets):
        at = file(core, y, (x + d) % 4)
        out.arrived(rowx.at[at], row_sem.at[at], place)
        for to in targets:
            out.send(rowx.at[at], rowx.at[at], row_sem.at[at], to)

    def take_col(slot, targets):
        out.arrived(colx.at[slot], col_sem.at[slot], place)
        for to in targets:
            out.send(colx.at[slot], colx.at[slot], col_sem.at[slot], to)

    def four(c, y):
        return rowx.at[pl.ds(file(c, y, 0), 4)]

    def give(y):
        out.send(four(core, y), four(core, y), core_sem.at[y], place.sibling)

    def expand_row(c, y, d):
        expand(rowx.at[file(c, y, (x + d) % 4)], ex, place.col_of(y, (x + d) % 4, c))

    take_row(1 - yl, 0, [place.xs[0], place.xs[2], place.xs[1]])
    take_col(place.row_of(z, 1 - yh), [place.zs[0], place.zs[2], place.zs[1]])
    for d in (1, 3, 2):
        take_row(yl, d, [])
    give(yl)
    expand_row(core, 1 - yl, 0)
    expand(colx.at[place.row_of(z, 1 - yh)], xc, place.row_of(z, 1 - yh))
    for d in (1, 3, 2):
        expand_row(core, yl, d)
    for d in (1, 3, 2):
        take_col(place.row_of((z + d) % 4, yh), [])
        expand(colx.at[place.row_of((z + d) % 4, yh)], xc, place.row_of((z + d) % 4, yh))
    for d in (1, 3, 2):
        take_row(1 - yl, d, [])
    give(1 - yl)
    out.arrived(four(1 - core, yl), core_sem.at[yl], place)
    for d in (0, 1, 2, 3):
        expand_row(1 - core, yl, d)
    for d in (1, 3, 2):
        expand_row(core, 1 - yl, d)
    for d in (1, 3, 2):
        take_col(place.row_of((z + d) % 4, 1 - yh), [])
        expand(colx.at[place.row_of((z + d) % 4, 1 - yh)], xc, place.row_of((z + d) % 4, 1 - yh))
    out.arrived(four(1 - core, 1 - yl), core_sem.at[1 - yl], place)
    for d in (0, 1, 2, 3):
        expand_row(1 - core, 1 - yl, d)
    out.finish()
    for load in loads:
        load.wait()


def gather(count, row_index, col_index, basis_vectors, block_values):
    pairs = block_values.reshape(GROUPS, 4, 2, 32, 128).transpose(0, 3, 1, 2, 4)
    ex, xc, vals, racc, cacc, to_rows, to_cols = pl.pallas_call(
        gather_kernel,
        out_shape=(
            pltpu.VMEM(((NB_ROW + 1) * 8, 128), F32),
            pltpu.VMEM(((NB_COL + 1) * 8, 128), F32),
            pltpu.VMEM((GROUPS, 4, 32, 2, 128), BF16),
            pltpu.VMEM(((NB_ROW + 1) * 8, 128), F32),
            pltpu.VMEM(((NB_COL + 1) * 8, 128), F32),
            pltpu.VMEM((16, 128), I32),
            pltpu.VMEM((16, 128), I32),
        ),
        in_specs=[SMEM, ANY, ANY, ANY, ANY],
        out_specs=(VMEM,) * 7,
        scratch_shapes=[
            pltpu.VMEM((16, 128), I32),
            pltpu.VMEM((16, 128), I32),
            pltpu.VMEM((N_COL, NVEC, PIECE), BF16),
            pltpu.VMEM((N_ROW, NVEC, PIECE), BF16),
            pltpu.SemaphoreType.DMA((3,)),
            pltpu.SemaphoreType.DMA((4,)),
            pltpu.SemaphoreType.DMA((16,)),
            pltpu.SemaphoreType.DMA((N_COL,)),
            pltpu.SemaphoreType.DMA((N_ROW,)),
            pltpu.SemaphoreType.DMA((2,)),
        ],
        compiler_params=pltpu.CompilerParams(collective_id=0, has_side_effects=True, vmem_limit_bytes=28 * MIB),
    )(count, row_index, col_index, basis_vectors, pairs)
    return to_rows.reshape(CAP), to_cols.reshape(CAP), ex, xc, vals.reshape(GROUPS, 256, 128), racc, cacc


def product_kernel(count_ref, row_at, col_at, ex, xc, vals, racc_in, cacc_in, racc, cacc):
    low, _ = lane_masks()
    lane = lax.broadcasted_iota(I32, (8, 128), 1)
    mine = [(lane // 64 == i // 2) & (lane % 2 == i % 2) for i in range(4)]
    half = [lane // 64 == i // 2 for i in range(4)]
    zero = jnp.zeros((8, 128), F32)

    def rows8(ref, s):
        return pl.ds(pl.multiple_of(ref[s], 8), 8)

    def operands(s, i):
        x = xc[rows8(col_at, s), :]
        left = jnp.concatenate([jnp.where(low, x, zero), jnp.where(low, zero, x)], axis=0).astype(BF16)
        x = ex[rows8(row_at, s), :]
        other = pltpu.roll(x, 1 if i % 2 else 127, 1)
        p0, p1 = (other, x) if i % 2 else (x, other)
        right = jnp.concatenate([jnp.where(mine[i], p0, zero), jnp.where(mine[i], p1, zero)], axis=0).astype(BF16)
        return left, right

    def group(t):
        pairs = [operands(t * 8 + s, s % 4) for s in range(8)]
        left = jnp.concatenate([p[0] for p in pairs], axis=0)
        right = jnp.concatenate([p[1] for p in pairs], axis=0)
        a = vals[t]
        forward = lax.dot_general(left, a, (((1,), (1,)), ((), ())), preferred_element_type=F32)
        wide = jnp.concatenate([a[:128], a[128:]], axis=1)
        backward = lax.dot_general(right, wide, (((1,), (0,)), ((), ())), preferred_element_type=F32)
        for s in range(8):
            to_row, to_col = rows8(row_at, t * 8 + s), rows8(col_at, t * 8 + s)
            h, i, par = s // 4 * 128, s * 16, s % 2
            same = forward[i + 8 * par:i + 8 * par + 8, h:h + 128]
            other = pltpu.roll(forward[i + 8 - 8 * par:i + 16 - 8 * par, h:h + 128], 127 if par else 1, 1)
            racc[to_row, :] += jnp.where(half[s % 4], jnp.where(mine[s % 4], same, other), zero)
            cacc[to_col, :] += jnp.where(low, backward[i:i + 8, h:h + 128], backward[i + 8:i + 16, h:h + 128])

    def step(u, carry):
        for k in range(UNROLL):
            group(u * UNROLL + k)
        return carry

    lax.fori_loop(0, (count_ref[0] + 8 * UNROLL - 1) // (8 * UNROLL), step, 0)


def products(count, row_at, col_at, ex, xc, vals, racc, cacc):
    return pl.pallas_call(
        product_kernel,
        out_shape=(pltpu.VMEM(racc.shape, F32), pltpu.VMEM(cacc.shape, F32)),
        in_specs=[SMEM, SMEM, SMEM, VMEM, VMEM, VMEM, VMEM, VMEM],
        out_specs=(VMEM, VMEM),
        input_output_aliases={6: 0, 7: 1},
        compiler_params=pltpu.CompilerParams(vmem_limit_bytes=4 * MIB),
    )(count, row_at, col_at, ex, xc, vals, racc, cacc)


def fold(acc, piece, put):
    low, _ = lane_masks()

    def step(i, top):
        for j in range(16):
            m = i * 16 + j
            e, o = acc[block_rows(piece * 64 + 2 * m), :], acc[block_rows(piece * 64 + 2 * m + 1), :]
            y = jnp.where(low, e, o) + pltpu.roll(jnp.where(low, o, e), 64, 1)
            top = jnp.maximum(top, jnp.abs(put(lane_tile(m), y)))
        return top

    return lax.fori_loop(0, 2, step, jnp.zeros((8, 128), F32))


def scale_of(code):
    return jnp.exp2(code * (1.0 / 256.0))


def to_wire(src, top, wire):
    some = top > 1e-33
    code = jnp.ceil(jnp.log2(jnp.where(some, top, 1.0)) * 256.0) + 1.0
    inverse = jnp.where(some, TOP / scale_of(code), 0.0)
    wire[:, lane_tile(16)] = jnp.concatenate([code, code], axis=0).astype(I32).astype(I16)

    def step(i, carry):
        for j in range(8):
            m = i * 8 + j
            halves = [jnp.round(src[:, lane_tile(m + 16 * k)] * inverse) for k in range(2)]
            wire[:, lane_tile(m)] = jnp.concatenate(halves, axis=0).astype(I32).astype(I16)
        return carry

    lax.fori_loop(0, 2, step, 0)


def add_up(put, terms, wires):
    scales = [scale_of(wire[:, lane_tile(16)].astype(I32).astype(F32)[:8]) * (1.0 / TOP) for wire in wires]

    def step(i, top):
        for j in range(4):
            m = i * 4 + j
            arrived = [wire[:, lane_tile(m)].astype(I32).astype(F32) for wire in wires]
            for k in range(2):
                at = lane_tile(m + 16 * k)
                total = None
                for term in terms:
                    total = term[:, at] if total is None else total + term[:, at]
                for a, scale in zip(arrived, scales):
                    total = total + a[8 * k:8 * k + 8] * scale
                put(at, total)
                top = jnp.maximum(top, jnp.abs(total))
        return top

    return lax.fori_loop(0, 4, step, jnp.zeros((8, 128), F32))


def scatter_kernel(racc, cacc, out_ref, for_core, from_core, row_part, col_part, sums,
                   out_wire, in_wire, send_sem, core_sem, wire_sem):
    place = Place()
    place.greet()
    yl, x, core, z, yh = place.yl, place.x, place.core, place.z, place.yh

    def write(ref):
        def put(at, y):
            ref[:, at] = y
            return y
        return put

    def remote(src, dst, sem, recv_sem, to):
        return pltpu.make_async_remote_copy(
            src_ref=src, dst_ref=dst, send_sem=send_sem.at[sem], recv_sem=recv_sem, device_id=to, device_id_type=MESH)

    def wire(at, to):
        return remote(out_wire.at[at], in_wire.at[at], at, wire_sem.at[at], to)

    def core_copy(k):
        return remote(for_core.at[k], from_core.at[k], 14 + k, core_sem.at[k], place.sibling)

    def receive(at):
        wire(at, place.sibling).wait_recv()

    def order(k):
        last, j = k // 6, k % 3
        return (1 - last) * (1 - k // 3) + last * (7 - k), (1 - last) * (2 - j + 3 * (j // 2))

    def for_sibling(k):
        h, d = order(k)
        fold(racc, place.col_of(h * (1 - yl) + (1 - h) * yl, (x + d) % 4, 1 - core), write(for_core.at[k]))

    def columns(k):
        h, d = order(k)
        return h, d, fold(cacc, place.row_of((z + d) % 4, h * (1 - yh) + (1 - h) * yh), write(col_part.at[d, h]))

    def rows(k):
        h, d = order(k)
        core_copy(k).wait_recv()

        def put(at, y):
            y = y + from_core[k, :, at]
            row_part[d, h, :, at] = y
            return y

        return h, d, fold(racc, place.col_of(h * (1 - yl) + (1 - h) * yl, (x + d) % 4, core), put)

    for_sibling(0)
    place.wait_greetings()
    core_copy(0).start()
    for_sibling(1)
    core_copy(1).start()

    def each(k, carry):
        h, d, top = columns(k)
        at = 6 + (d - 1) * 2 + h
        to_wire(col_part.at[d, h], top, out_wire.at[at])
        wire(at, (place.row_of((z + d) % 4, yh), place.col)).start()
        for_sibling(k + 2)
        core_copy(k + 2).start()
        h, d, top = rows(k)
        at = (d - 1) * 2 + h
        to_wire(row_part.at[d, h], top, out_wire.at[at])
        wire(at, (place.row, place.col_of(yl, (x + d) % 4, core))).start()
        return carry

    lax.fori_loop(0, 6, each, 0)

    def keep(k, carry):
        columns(k)
        rows(k)
        return carry

    lax.fori_loop(6, 8, keep, 0)
    for d in (1, 3, 2):
        receive(6 + (d - 1) * 2 + 1)
    top = add_up(write(sums.at[1]), [col_part.at[0, 1]], [in_wire.at[6 + (d - 1) * 2 + 1] for d in (1, 3, 2)])
    to_wire(sums.at[1], top, out_wire.at[13])
    wire(13, place.y_hi).start()
    for d in (1, 3, 2):
        receive((d - 1) * 2 + 1)
    top = add_up(write(sums.at[0]), [row_part.at[0, 1]], [in_wire.at[(d - 1) * 2 + 1] for d in (1, 3, 2)])
    to_wire(sums.at[0], top, out_wire.at[12])
    wire(12, place.y_lo).start()
    for d in (1, 3, 2):
        receive((d - 1) * 2)
        receive(6 + (d - 1) * 2)
    add_up(write(sums.at[2]), [row_part.at[0, 0], col_part.at[0, 0]],
           [in_wire.at[(d - 1) * 2] for d in (1, 3, 2)] + [in_wire.at[6 + (d - 1) * 2] for d in (1, 3, 2)])
    receive(13)
    receive(12)
    add_up(write(out_ref), [sums.at[2]], [in_wire.at[13], in_wire.at[12]])

    def sent_wire(at, carry):
        wire(at, place.sibling).wait_send()
        return carry

    def sent_core(k, carry):
        core_copy(k).wait_send()
        return carry

    lax.fori_loop(0, 14, sent_wire, 0)
    lax.fori_loop(0, 8, sent_core, 0)


def scatter(racc, cacc):
    piece, wire = (NVEC, PIECE), (2 * NVEC, PIECE // 2 + 128)
    return pl.pallas_call(
        scatter_kernel,
        out_shape=jax.ShapeDtypeStruct(piece, F32),
        in_specs=[VMEM, VMEM],
        out_specs=VMEM,
        scratch_shapes=[
            pltpu.VMEM((8,) + piece, F32), pltpu.VMEM((8,) + piece, F32),
            pltpu.VMEM((4, 2) + piece, F32), pltpu.VMEM((4, 2) + piece, F32), pltpu.VMEM((3,) + piece, F32),
            pltpu.VMEM((14,) + wire, I16), pltpu.VMEM((14,) + wire, I16),
            pltpu.SemaphoreType.DMA((22,)),
            pltpu.SemaphoreType.DMA((8,)), pltpu.SemaphoreType.DMA((14,)),
        ],
        compiler_params=pltpu.CompilerParams(collective_id=1, has_side_effects=True, vmem_limit_bytes=8 * MIB),
    )(racc, cacc)


def body(basis_vectors, block_values, blk_row, blk_col, block_count):
    count = block_count.reshape(1)
    row_at, col_at, ex, xc, vals, racc, cacc = gather(
        count, blk_row.reshape(16, 128), blk_col.reshape(16, 128), basis_vectors, block_values.reshape(CAP, BLK * BLK))
    racc, cacc = products(count, row_at, col_at, ex, xc, vals, racc, cacc)
    return scatter(racc, cacc)


def solution(mesh):
    return jax.shard_map(
        body,
        mesh=mesh,
        in_specs=(
            P(None, ("row", "col")),
            P("row", "col", None, None),
            P("row", "col", None),
            P("row", "col", None),
            P("row", "col"),
        ),
        out_specs=P(None, ("row", "col")),
        check_vma=False,
    )
```
